128 devices in a mesh: rep: 4 (over z), exp: 32 (over y, x, core).
Axes of the slice: x: 4, y: 4, z: 4, core: 2. Of those that a mesh axis runs over, the one named last changes fastest.
Arguments:
- hidden_in: bfloat16 [32768, 768], P(('rep', 'exp')), may hold values from -6 to 6
- doc_ids: int32 [32768], P(('rep', 'exp')), may hold values from 0 to 127, as said below
- routes: int32 [32768, 1], P(('rep', 'exp')), may hold values from 0 to 31; in each aligned block of 256 rows (0 to 255, 256 to 511, ...) at most 16 rows name the same one
- attn_gain: bfloat16 [768], P('exp'), may hold values from 0.5 to 1.5
- w_query: bfloat16 [768, 768], P('exp'), may hold values from -0.21875 to 0.21875
- w_key: bfloat16 [768, 768], P('exp'), may hold values from -0.21875 to 0.21875
- w_value: bfloat16 [768, 768], P('exp'), may hold values from -0.21875 to 0.21875
- w_out: bfloat16 [768, 768], P('exp'), may hold values from -0.625 to 0.625
- rel_bias: bfloat16 [32, 12], P('exp'), may hold values from -4 to 4
- ffn_gain: bfloat16 [768], P('exp'), may hold values from 0.5 to 1.5
- w_router: bfloat16 [768, 32], P('exp'), may hold values from -0.109375 to 0.109375
- w_in: bfloat16 [32, 768, 3072], P('exp'), may hold values from -0.21875 to 0.21875
- w_down: bfloat16 [32, 3072, 768], P('exp'), may hold values from -6 to 6
- out_grad: bfloat16 [32768, 768], P(('rep', 'exp')), may hold values from -6 to 6
Outputs:
- block_out: bfloat16 [32768, 768], P(('rep', 'exp'))
- grad_in: float32 [32768, 768], P(('rep', 'exp'))
- grad_attn_gain: float32 [768], P('exp')
- grad_query: float32 [768, 768], P('exp')
- grad_key: float32 [768, 768], P('exp')
- grad_value: float32 [768, 768], P('exp')
- grad_out: float32 [768, 768], P('exp')
- grad_rel_bias: float32 [32, 12], P('exp')
- grad_ffn_gain: float32 [768], P('exp')
- grad_router: float32 [768, 32], P('exp')
- grad_w_in: float32 [32, 768, 3072], P('exp', None, 'rep')
- grad_w_down: float32 [32, 3072, 768], P('exp', 'rep')
The draws below stay inside these ranges and needn't reach their ends.
Inputs may be any that keep to these rules, and one draw needn't show every extreme that they name: `doc_ids`: within each block of 256 consecutive tokens (one device's) the ids start at 0 and never fall; a sequence is a run of equal ids and starts at an even position of its block; the first block is a single sequence. `routes`: among the tokens of one device no expert is named more than 16 times.
All inputs are finite; a program needn't handle non-finite values.
Results may differ from the reference program's by a relative error of at most 0.028.
Values may be sent and summed in bfloat16 or wider, within the bound.
No kernel may reach another device: no remote copies, remote signals or barrier semaphores. Data moves between devices by JAX's collectives and lax.ppermute only.
A program may use at most 128 MiB of HBM per device.

```python
import math
import jax
import jax.numpy as jnp
import numpy as np
from jax import lax

HEADS = 12
HEAD_DIM = 64
D = 768
FF = 3072
BUCKETS = 32
TOK_DEV = 256
EXPERTS = 32
CAP = 16
TOKENS = 32768


def draw_doc_ids(key, part):
    key = jax.random.fold_in(key, 7)
    blocks = TOKENS // TOK_DEV
    first, second = jax.random.split(key)
    power = jax.random.randint(first, (blocks, 1), 1, 6)
    odds = jnp.left_shift(jnp.ones_like(power), power)
    starts = jax.random.randint(second, (blocks, TOK_DEV), 0, odds) == 0
    column = jnp.arange(TOK_DEV)[None, :]
    row = jnp.arange(blocks)[:, None]
    even = column % 2 == 0
    starts = (starts | (row == blocks - 1)) & even & (column > 0) & (row != 0)
    return jnp.cumsum(starts.astype(jnp.int32), axis=1).astype(jnp.int32).reshape(TOKENS)


def level_of(own_key, shape, shards, least, top_value):
    level, own = 1.0, jax.random.fold_in(own_key, 6)
    for dim, shards_of in shards:
        draws = jnp.exp(jax.random.uniform(jax.random.fold_in(own, dim), (shards_of,), jnp.float32, least / len(shards), top_value / len(shards)))
        level = level * jnp.repeat(draws, shape[dim] // shards_of).reshape([-1 if axis == dim else 1 for axis in range(len(shape))])
    return level


def shared_out(own_key, own, number, rows, number_of, top, bound, slope):
    order = jax.random.permutation(own_key, number_of)
    heavy_load, ordinary = shares(number_of, rows * top, bound, slope, True), shares(number_of, rows * top, bound, slope, False)
    places = jnp.arange(number_of)

    def named(lengths, offset_by):
        used = int((lengths > 0).sum())
        fixed = max(1, used // 4)
        moved = fixed + (places - fixed + offset_by * (used - fixed)) % max(1, number_of - fixed)
        return jnp.zeros((number_of,), jnp.int32).at[order[jnp.where(places < fixed, places, moved)]].set(jnp.asarray(lengths, jnp.int32))

    lengths = jnp.where(number % 4 == 0, named(heavy_load, number // 4), named(ordinary, number - number // 4 - 1))
    mixed = jax.random.permutation(jax.random.fold_in(own, 3), number_of)
    giver, taker = mixed[0:number_of // 2 * 2:2], mixed[1:number_of // 2 * 2:2]
    margin = jnp.minimum(lengths[giver] - 1, bound - lengths[taker]) // 2
    margin = jnp.where((giver == order[0]) | (taker == order[0]) | (lengths[taker] == 0), 0, jnp.maximum(margin, 0))
    moved = jax.random.randint(jax.random.fold_in(own, 4), (number_of // 2,), 0, 1 << 20) % (margin + 1)
    lengths = lengths.at[giver].add(-moved).at[taker].add(moved)
    members = jnp.searchsorted(jnp.cumsum(lengths), jnp.arange(rows * top), side="right").astype(jnp.int32)
    listing = members.reshape(top, rows).T
    listing = listing[jax.random.permutation(jax.random.fold_in(own, 1), rows)]
    offset_by = jax.random.randint(jax.random.fold_in(own, 2), (rows, 1), 0, top)
    return jnp.take_along_axis(listing, (jnp.arange(top)[None, :] + offset_by) % top, axis=1)


def shares(count, total, reach, skew, full):
    portions = [(1 << 20) // math.isqrt(rank ** skew) + 1 for rank in range(1, count + 1)]
    largest = reach if full else min(reach, max(-(-total // count), total * portions[0] // sum(portions)))
    least = 1 if total - largest >= count - 1 else 0
    counts, surplus = [largest] + [least] * (count - 1), total - largest - least * (count - 1)
    while surplus > 0:
        movable = [i for i in range(1, count) if counts[i] < largest] or [i for i in range(1, count) if counts[i] < reach]
        whole, budget = sum([portions[i] for i in movable]), surplus
        for i in movable:
            extra = min(reach - counts[i], max(1, budget * portions[i] // whole), surplus)
            counts[i] = counts[i] + extra
            surplus = surplus - extra
    return np.array(counts)


def normal_values(stream_key, dims, width, reach, cuts=(), kind=jnp.bfloat16):
    result = jax.random.normal(stream_key, dims, jnp.float32) * width
    if len(cuts) > 0:
        result = level_of(stream_key, dims, cuts, -0.22, 0.18) * result
    return jnp.clip(result, min=-reach, max=reach).astype(kind)


def setup_inputs(seed: int = 0) -> dict:
    splits = jax.random.split(jax.random.key(seed), 15)
    hidden_in = normal_values(splits[0], (TOKENS, D), 1.0, 6.0, ((0, 128),))
    doc_ids = draw_doc_ids(jax.random.fold_in(splits[14], 71), 0)
    routes_keys = jax.random.split(jax.random.fold_in(splits[2], 1), TOKENS // TOK_DEV)
    routes_turns = jax.random.permutation(jax.random.fold_in(splits[2], 3), TOKENS // TOK_DEV)
    routes = jax.vmap(lambda own, number: shared_out(jax.random.fold_in(splits[2], 2), own, number, TOK_DEV, EXPERTS, 1, CAP, 2))(routes_keys, routes_turns).reshape((TOKENS, 1))
    attn_gain = jnp.clip(1.0 + 0.1 * jax.random.normal(splits[3], (D,), jnp.float32), 0.5, 1.5).astype(jnp.bfloat16)
    w_query = normal_values(splits[4], (D, D), D ** -0.5, 0.21875, ((0, 32),))
    w_key = normal_values(splits[5], (D, D), D ** -0.5, 0.21875, ((0, 32),))
    w_value = normal_values(splits[6], (D, D), D ** -0.5, 0.21875, ((0, 32),))
    w_out = normal_values(splits[7], (D, D), (D // 8) ** -0.5, 0.625, ((0, 32),))
    rel_bias = normal_values(splits[8], (BUCKETS, HEADS), 1.0, 4.0, ((0, 32),))
    ffn_gain = jnp.clip(1.0 + 0.1 * jax.random.normal(splits[9], (D,), jnp.float32), 0.5, 1.5).astype(jnp.bfloat16)
    w_router = normal_values(splits[10], (D, EXPERTS), (4 * D) ** -0.5, 0.109375, ((0, 32),))
    w_in = normal_values(splits[11], (EXPERTS, D, FF), D ** -0.5, 0.21875, ((0, 32),))
    w_down = normal_values(splits[12], (EXPERTS, FF, D), (max(1, FF // (4 * EXPERTS * EXPERTS))) ** -0.5, 6.0, ((0, 32),))
    out_grad = normal_values(splits[13], (TOKENS, D), 1.0, 6.0, ((0, 128),))
    return {"hidden_in": hidden_in, "doc_ids": doc_ids, "routes": routes, "attn_gain": attn_gain, "w_query": w_query, "w_key": w_key, "w_value": w_value, "w_out": w_out, "rel_bias": rel_bias, "ffn_gain": ffn_gain, "w_router": w_router, "w_in": w_in, "w_down": w_down, "out_grad": out_grad}


@jax.custom_vjp
def low(v):
    return lax.optimization_barrier(v.astype(jnp.bfloat16)).astype(jnp.float32)

@jax.custom_vjp
def low_back(v):
    return v

def low_keep(v):
    return (low(v), None)

def low_pass(kept, grad):
    return (grad,)

def back_keep(v):
    return (v, None)

def back_low(kept, grad):
    return (low(grad),)
low.defvjp(low_keep, low_pass)
low_back.defvjp(back_keep, back_low)
eps = 1e-06
reach_marks = (12, 16, 23, 32, 46, 64, 91)
big_negative = -1000000000.0

def bucket_index(length):
    position = jnp.arange(length, dtype=jnp.int32)
    relative = position[None, :] - position[:, None]
    distance = jnp.abs(relative)
    far_bucket = 8 + sum(((distance >= reach_mark).astype(jnp.int32) for reach_mark in reach_marks))
    return jnp.where(distance < 8, distance, far_bucket) + 16 * (relative > 0).astype(jnp.int32)

def matmul_hi(left, right):
    return jnp.dot(left, right, precision=lax.Precision.HIGHEST)

def rms_norm(values_in, gain):
    return values_in * lax.rsqrt(lax.optimization_barrier(jnp.mean(values_in * values_in, axis=-1, keepdims=True)) + eps) * gain

def reference(hidden_in, doc_ids, routes, attn_gain, w_query, w_key, w_value, w_out, rel_bias, ffn_gain, w_router, w_in, w_down, out_grad):
    blocks = TOKENS // TOK_DEV
    bucket_hot = jax.nn.one_hot(bucket_index(TOK_DEV), BUCKETS, dtype=jnp.float32)
    doc_blocks = doc_ids.reshape(blocks, TOK_DEV)
    route_flat = routes[:, 0]
    chosen_int = (route_flat[:, None] == jnp.arange(EXPERTS, dtype=jnp.int32)[None, :]).astype(jnp.int32)
    chosen_blocks = chosen_int.reshape(blocks, TOK_DEV, EXPERTS)
    slot_rank = lax.optimization_barrier(jnp.sum((jnp.cumsum(chosen_blocks, axis=1) - chosen_blocks) * chosen_blocks, axis=-1)).reshape(TOKENS)
    device_of = jnp.arange(TOKENS, dtype=jnp.int32) // TOK_DEV
    slot_index = (route_flat * (blocks * CAP) + device_of * CAP + slot_rank).astype(jnp.int32)
    chosen = chosen_int.astype(jnp.float32)
    score_scale = HEAD_DIM ** (-0.5)

    def forward(residual_in, gain_attn, query_weight, key_weight, value_weight, out_weight, bias_table, gain_ffn, router_weight, in_weights, down_weights):
        attn_input = low(rms_norm(residual_in, gain_attn))
        queries = low_back(low(matmul_hi(attn_input, query_weight)))
        keys_all = low_back(low(matmul_hi(attn_input, key_weight)))
        values_all = low_back(low(matmul_hi(attn_input, value_weight)))

        def attend(packed):
            block_q, block_k, block_v, block_ids = packed
            raw_scores = score_scale * jnp.einsum('ihd,jhd->hij', block_q, block_k, precision=lax.Precision.HIGHEST)
            raw_scores = raw_scores + jnp.einsum('ijb,bh->hij', bucket_hot, bias_table, precision=lax.Precision.HIGHEST)
            scores = low_back(raw_scores)
            same_doc = block_ids[:, None] == block_ids[None, :]
            scores = jnp.where(same_doc[None], scores, big_negative)
            weights = low(jax.nn.softmax(scores, axis=-1))
            return low_back(low(jnp.einsum('hij,jhd->ihd', weights, block_v, precision=lax.Precision.HIGHEST)))
        shaped = (blocks, TOK_DEV, HEADS, HEAD_DIM)
        attended = lax.map(jax.checkpoint(attend), (queries.reshape(shaped), keys_all.reshape(shaped), values_all.reshape(shaped), doc_blocks))
        attended = attended.reshape(TOKENS, D)
        after_attn = residual_in + low_back(matmul_hi(attended, out_weight))
        ffn_input = low(rms_norm(after_attn, gain_ffn))
        logits = low_back(matmul_hi(ffn_input, router_weight))
        gate_prob = lax.optimization_barrier(jnp.sum(jax.nn.softmax(logits, axis=-1) * chosen, axis=-1))
        dispatched = jnp.zeros((EXPERTS * blocks * CAP, D), jnp.float32).at[slot_index].set(ffn_input)
        dispatched = low_back(dispatched).reshape(EXPERTS, blocks * CAP, D)

        def expert(packed):
            slot_rows, in_weight, down_weight = packed
            pre_act = low_back(matmul_hi(slot_rows, in_weight))
            activated = low(jax.nn.gelu(pre_act))
            return low_back(low(matmul_hi(activated, down_weight)))
        produced = lax.map(jax.checkpoint(expert), (dispatched, in_weights, down_weights)).reshape(EXPERTS * blocks * CAP, D)
        return after_attn + gate_prob[:, None] * produced[slot_index]
    floats = tuple((array_in.astype(jnp.float32) for array_in in (hidden_in, attn_gain, w_query, w_key, w_value, w_out, rel_bias, ffn_gain, w_router, w_in, w_down)))
    block_out, pull_back = jax.vjp(forward, *floats)
    grads = pull_back(out_grad.astype(jnp.float32))
    return (block_out.astype(jnp.bfloat16), grads[0], grads[1], grads[2], grads[3], grads[4], grads[5], grads[6], grads[7], grads[8], grads[9], grads[10])
```

```python
import jax
import jax.numpy as jnp
from jax import lax
from jax.experimental import pallas as pl
from jax.experimental.pallas import tpu as pltpu
from jax.sharding import PartitionSpec as P

HEADS = 12
HEAD_DIM = 64
BUCKETS = 32
D = 768
FF = 3072
TOK = 256
EXPERTS = 32
CAP = 16
SLOTS = EXPERTS * CAP
QKV = 3 * D
WIDE1 = QKV + 256
WIDE2 = D + 256

eps = 1e-06
reach_marks = (12, 16, 23, 32, 46, 64, 91)
big_negative = -1000000000.0
score_scale = HEAD_DIM ** (-0.5)

f32 = jnp.float32
bf16 = jnp.bfloat16
HIGHEST = lax.Precision.HIGHEST

NN = ((1,), (0,))
NT = ((1,), (1,))
TN = ((0,), (0,))

SWAP = [(i, i ^ 1) for i in range(32)]


def x_shift(step):
    return [
        (y * 8 + x * 2 + c, y * 8 + ((x + step) % 4) * 2 + c)
        for y in range(4)
        for x in range(4)
        for c in range(2)
    ]


def y_shift(step):
    return [
        (y * 8 + x * 2 + c, ((y + step) % 4) * 8 + x * 2 + c)
        for y in range(4)
        for x in range(4)
        for c in range(2)
    ]


def z_shift(step):
    return [(i, (i + step) % 4) for i in range(4)]


def on_exp(value, pairs):
    return lax.ppermute(value, "exp", pairs)


def dot(left, right, dims, precision=None):
    return lax.dot_general(
        left, right, (dims, ((), ())), precision=precision, preferred_element_type=f32
    )


def call(body, outs, *args, scratch=(), smem=1, flops=0, bytes_accessed=0, vmem=48):
    specs = [
        pl.BlockSpec(memory_space=pltpu.SMEM if i < smem else pltpu.VMEM)
        for i in range(len(args))
    ]
    return pl.pallas_call(
        body,
        out_shape=[jax.ShapeDtypeStruct(shape, kind) for shape, kind in outs],
        in_specs=specs,
        out_specs=[pl.BlockSpec(memory_space=pltpu.VMEM) for _ in outs],
        scratch_shapes=list(scratch),
        compiler_params=pltpu.CompilerParams(vmem_limit_bytes=vmem * 1024 * 1024),
        cost_estimate=pl.CostEstimate(
            flops=flops, bytes_accessed=bytes_accessed, transcendentals=0
        ),
    )(*args)


def gather_pieces(shard, core):
    half, quarter = shard.shape[1] // 2, shard.shape[1] // 4
    low, high = shard[:, :half], shard[:, half:]
    mine = jnp.where(core == 0, low, high)
    other = jnp.where(core == 0, high, low)
    got = on_exp(other, SWAP)
    chip = jnp.where(
        core == 0, jnp.concatenate([mine, got]), jnp.concatenate([got, mine])
    )
    first, second = chip[:, :quarter], chip[:, quarter:]
    first = jnp.stack([first] + [on_exp(first, x_shift(-k)) for k in (1, 2, 3)])
    second = jnp.stack([second] + [on_exp(second, y_shift(-k)) for k in (1, 2, 3)])
    pieces = [first] + [on_exp(first, y_shift(-k)) for k in (1, 2, 3)]
    pieces += [second] + [on_exp(second, x_shift(-k)) for k in (1, 2, 3)]
    return pieces + [on_exp(piece, SWAP) for piece in pieces]


def row_of(pos, ky, kx):
    chip = ((pos[0] + ky) & 3) * 4 + ((pos[1] + kx) & 3)
    return pl.multiple_of(chip * 48, 16)


def place_pieces(pos, pieces, whole):
    quarter = whole.shape[1] // 4
    for side in range(2):
        owner = pos[2] if side == 0 else 1 - pos[2]
        for way in range(2):
            column = pl.multiple_of(owner * (2 * quarter) + way * quarter, 128)
            for outer in range(4):
                for inner in range(4):
                    ky, kx = (outer, inner) if way == 0 else (inner, outer)
                    whole[pl.ds(row_of(pos, ky, kx), 48), pl.ds(column, quarter)] = pieces[
                        side * 8 + way * 4 + outer
                    ][inner]


def arrange_pieces(pos, whole, keep, send):
    quarter = whole.shape[1] // 4
    for side in range(2):
        owner = pos[2] if side == 0 else 1 - pos[2]
        target = keep if side == 0 else send
        for way in range(2):
            column = pl.multiple_of(owner * (2 * quarter) + way * quarter, 128)
            for outer in range(4):
                for inner in range(4):
                    ky, kx = (inner, outer) if way == 0 else (outer, inner)
                    target[way * 4 + outer, inner] = whole[
                        pl.ds(row_of(pos, ky, kx), 48), pl.ds(column, quarter)
                    ]


def sum_cores(keep, got, *outs):
    for k in range(8):
        outs[k][...] = (keep[k].astype(f32) + got[k].astype(f32)).astype(bf16)


def sum_first(*refs):
    ins, outs = refs[:8], refs[8:]
    for way in range(2):
        for k in range(4):
            total = ins[way * 4][k].astype(f32)
            for j in (1, 2, 3):
                total = total + ins[way * 4 + j][k].astype(f32)
            outs[way * 4 + k][...] = total.astype(bf16)


def sum_second(pos, *refs):
    ins, (keep, send) = refs[:8], refs[8:]
    quarter = keep.shape[1] // 2
    for way in range(2):
        total = ins[way * 4][...].astype(f32)
        for j in (1, 2, 3):
            total = total + ins[way * 4 + j][...].astype(f32)
        low, high = total[:24], total[24:]
        columns = slice(way * quarter, (way + 1) * quarter)
        keep[:, columns] = jnp.where(pos[2] == 0, low, high).astype(bf16)
        send[:, columns] = jnp.where(pos[2] == 0, high, low).astype(bf16)


def reduce_pieces(pos, core, keep, send):
    quarter = keep.shape[3]
    got = on_exp(send, SWAP)
    parts = call(sum_cores, [((4, 48, quarter), bf16)] * 8, keep, got, smem=0)
    parts = (
        [parts[0]]
        + [on_exp(parts[k], x_shift(k)) for k in (1, 2, 3)]
        + [parts[4]]
        + [on_exp(parts[4 + k], y_shift(k)) for k in (1, 2, 3)]
    )
    parts = call(sum_first, [((48, quarter), bf16)] * 8, *parts, smem=0)
    parts = (
        [parts[0]]
        + [on_exp(parts[k], y_shift(k)) for k in (1, 2, 3)]
        + [parts[4]]
        + [on_exp(parts[4 + k], x_shift(k)) for k in (1, 2, 3)]
    )
    keep, send = call(sum_second, [((24, 2 * quarter), bf16)] * 2, pos, *parts)
    got = on_exp(send, SWAP)
    own = jnp.where(
        core == 0,
        jnp.concatenate([keep, got], axis=1),
        jnp.concatenate([got, keep], axis=1),
    )
    beside = lax.ppermute(own, "rep", [(i, i ^ 1) for i in range(4)])
    pair = (own.astype(f32) + beside.astype(f32)).astype(bf16)
    across = lax.ppermute(pair, "rep", [(i, 3 - i) for i in range(4)])
    return pair.astype(f32) + across.astype(f32)


def diagonal_buckets():
    lane = lax.broadcasted_iota(jnp.int32, (8, 512), 1)
    row = lax.broadcasted_iota(jnp.int32, (8, 512), 0)
    relative = lane - row - 255
    distance = jnp.abs(relative)
    far = jnp.full((8, 512), 8, jnp.int32)
    for mark in reach_marks:
        far = far + (distance >= mark).astype(jnp.int32)
    return jnp.where(distance < 8, distance, far) + jnp.where(relative > 0, 16, 0)


def bucket_hot(buckets, row):
    which = lax.broadcasted_iota(jnp.int32, (BUCKETS, 512), 0)
    return (which == jnp.broadcast_to(buckets[row : row + 1], (BUCKETS, 512))).astype(f32)


def owner_rows():
    row = lax.broadcasted_iota(jnp.int32, (BUCKETS, D), 0)
    column = lax.broadcasted_iota(jnp.int32, (BUCKETS, D), 1)
    return (column == row * 24).astype(bf16)


def lane_zero():
    return (lax.broadcasted_iota(jnp.int32, (8, 128), 1) == 0).astype(bf16)


def inverse_rms(values):
    return lax.rsqrt(jnp.mean(values * values, axis=-1, keepdims=True) + eps)


def attention_forward(pos, x_ref, doc_col, doc_row, *refs):
    pieces = refs[:16]
    weights, attn_in, projected, probs, attended, base = refs[16:]
    place_pieces(pos, pieces, weights)
    gain = dot(lane_zero(), weights[:, QKV : QKV + 128], NT)[0:1]
    table = dot(weights[:, QKV + 128 : QKV + 256], owner_rows(), ((0,), (1,)))[0:16]
    buckets = diagonal_buckets()
    for row in range(8):
        base[:, row, :] = dot(table.astype(bf16), bucket_hot(buckets, row).astype(bf16), NN)
    x = x_ref[...].astype(f32)
    attn_in[...] = (x * inverse_rms(x) * gain).astype(bf16)
    for part in range(3):
        columns = slice(part * D, (part + 1) * D)
        projected[:, columns] = dot(attn_in[...], weights[:, columns], NN).astype(bf16)
    same = doc_col[...] == doc_row[...]
    left = lax.broadcasted_iota(jnp.int32, (TOK, 128), 1) < 64

    def pair_step(pair, carry):
        start = pair * 128
        queries = projected[:, pl.ds(pl.multiple_of(start, 128), 128)]
        keys = projected[:, pl.ds(pl.multiple_of(start + D, 128), 128)]
        values = projected[:, pl.ds(pl.multiple_of(start + 2 * D, 128), 128)]
        results = []
        for side in range(2):
            mine = left if side == 0 else jnp.logical_not(left)
            own = jnp.where(mine, queries, jnp.zeros_like(queries))
            diagonal = base[2 * pair + side]
            bias = jnp.concatenate(
                [pltpu.roll(diagonal, 257 + 8 * g, 1)[:, :256] for g in range(32)], axis=0
            )
            scores = jnp.where(same, score_scale * dot(own, keys, NT) + bias, big_negative)
            top = jnp.max(scores, axis=-1, keepdims=True)
            grown = jnp.exp(scores - top)
            share = grown * (1.0 / jnp.sum(grown, axis=-1, keepdims=True))
            share = share.astype(bf16)
            probs[2 * pair + side] = share
            results.append(dot(share, values, NN))
        attended[:, pl.ds(pl.multiple_of(start, 128), 128)] = jnp.where(
            left, results[0], results[1]
        ).astype(bf16)
        return carry

    lax.fori_loop(0, HEADS // 2, pair_step, 0)


def route_forward(pos, x_ref, routes, out_grad, attended, *refs):
    pieces = refs[:16]
    weights, after, ffn_in, router, gate, placer, outbound, grad_outbound = refs[16:]
    place_pieces(pos, pieces, weights)
    gain = dot(lane_zero(), weights[:, D + 128 : D + 256], NT)[0:1]
    after_attn = x_ref[...].astype(f32) + dot(attended[...], weights[:, :D], NN)
    after[...] = after_attn
    ffn_input = (after_attn * inverse_rms(after_attn) * gain).astype(bf16)
    ffn_in[...] = ffn_input
    lane = lax.broadcasted_iota(jnp.int32, (TOK, 128), 1)
    logits = dot(ffn_input, weights[:, D : D + 128], NN)
    logits = jnp.where(lane < EXPERTS, logits, -1e30)
    grown = jnp.exp(logits - jnp.max(logits, axis=-1, keepdims=True))
    share = grown / jnp.sum(grown, axis=-1, keepdims=True)
    router[...] = share
    chosen = routes[...] == lane
    gates = jnp.sum(jnp.where(chosen, share, 0.0), axis=-1, keepdims=True)
    gate[...] = gates
    earlier = (
        lax.broadcasted_iota(jnp.int32, (TOK, TOK), 1)
        < lax.broadcasted_iota(jnp.int32, (TOK, TOK), 0)
    ).astype(bf16)
    counts = dot(earlier, chosen.astype(bf16), NN)
    rank = jnp.sum(jnp.where(chosen, counts, 0.0), axis=-1, keepdims=True)
    slot = routes[...] * CAP + rank.astype(jnp.int32)
    placed = (slot == lax.broadcasted_iota(jnp.int32, (TOK, SLOTS), 1)).astype(bf16)
    placer[...] = placed
    outbound[...] = dot(placed, ffn_input, TN).astype(bf16)
    grads = (gates * out_grad[...].astype(f32)).astype(bf16)
    grad_outbound[...] = dot(placed, grads, TN).astype(bf16)


def gelu_parts(pre):
    square = pre * pre
    inner = 0.7978845608028654 * pre * (1.0 + 0.044715 * square)
    bend = jnp.tanh(inner)
    cdf = 0.5 * (1.0 + bend)
    slope = cdf + 0.5 * pre * (1.0 - bend * bend) * (
        0.7978845608028654 * (1.0 + 0.134145 * square)
    )
    return pre * cdf, slope


def expert_forward(rows, w_in, w_down, produced, slope, total):
    step = pl.program_id(0)

    @pl.when(step == 0)
    def _():
        total[...] = jnp.zeros_like(total)

    active, bend = gelu_parts(dot(rows[...], w_in[0], NN))
    slope[...] = bend.astype(bf16)
    total[...] += dot(active.astype(bf16), w_down[0], NN)

    @pl.when(step == pl.num_programs(0) - 1)
    def _():
        produced[...] = total[...].astype(bf16)


def expert_backward(grads, slope, w_in, w_down, grad_rows, total):
    step = pl.program_id(0)

    @pl.when(step == 0)
    def _():
        total[...] = jnp.zeros_like(total)

    grad_pre = dot(grads[...], w_down[0], NT) * slope[...].astype(f32)
    total[...] += dot(grad_pre.astype(bf16), w_in[0], NT)

    @pl.when(step == pl.num_programs(0) - 1)
    def _():
        grad_rows[...] = total[...].astype(bf16)


def expert_weights(pos, *refs):
    rows, grads = refs[:4], refs[4:8]
    w_in, w_down, grad_in, grad_down = refs[8:]
    for k in range(4):
        active, bend = gelu_parts(dot(rows[k][...], w_in[0], NN))
        grad_pre = (dot(grads[k][...], w_down[0], NT) * bend).astype(bf16)
        to_in = dot(rows[k][...], grad_pre, TN)
        to_down = dot(active.astype(bf16), grads[k][...], TN)
        if k == 0:
            grad_in[0] = to_in
            grad_down[0] = to_down
        else:
            grad_in[0] += to_in
            grad_down[0] += to_down


BLOCK = 512
WBLOCK = 256


def run_expert_forward(rows, w_in, w_down):
    whole = pl.BlockSpec((SLOTS, D), lambda f: (0, 0))
    return pl.pallas_call(
        expert_forward,
        grid=(FF // BLOCK,),
        in_specs=[
            whole,
            pl.BlockSpec((1, D, BLOCK), lambda f: (0, 0, f)),
            pl.BlockSpec((1, BLOCK, D), lambda f: (0, f, 0)),
        ],
        out_specs=[whole, pl.BlockSpec((SLOTS, BLOCK), lambda f: (0, f))],
        out_shape=[
            jax.ShapeDtypeStruct((SLOTS, D), bf16),
            jax.ShapeDtypeStruct((SLOTS, FF), bf16),
        ],
        scratch_shapes=[pltpu.VMEM((SLOTS, D), f32)],
        compiler_params=pltpu.CompilerParams(vmem_limit_bytes=40 * 1024 * 1024),
        cost_estimate=pl.CostEstimate(
            flops=4 * SLOTS * D * FF, bytes_accessed=14 * 1024 * 1024, transcendentals=0
        ),
    )(rows, w_in, w_down)


def run_expert_backward(grads, slope, w_in, w_down):
    whole = pl.BlockSpec((SLOTS, D), lambda f: (0, 0))
    return pl.pallas_call(
        expert_backward,
        grid=(FF // BLOCK,),
        in_specs=[
            whole,
            pl.BlockSpec((SLOTS, BLOCK), lambda f: (0, f)),
            pl.BlockSpec((1, D, BLOCK), lambda f: (0, 0, f)),
            pl.BlockSpec((1, BLOCK, D), lambda f: (0, f, 0)),
        ],
        out_specs=whole,
        out_shape=jax.ShapeDtypeStruct((SLOTS, D), bf16),
        scratch_shapes=[pltpu.VMEM((SLOTS, D), f32)],
        compiler_params=pltpu.CompilerParams(vmem_limit_bytes=40 * 1024 * 1024),
        cost_estimate=pl.CostEstimate(
            flops=4 * SLOTS * D * FF, bytes_accessed=14 * 1024 * 1024, transcendentals=0
        ),
    )(grads, slope, w_in, w_down)


def run_expert_weights(group, rows, grads, w_in, w_down):
    whole = pl.BlockSpec((SLOTS, D), lambda f, g: (0, 0))
    steps = D // WBLOCK
    return pl.pallas_call(
        expert_weights,
        grid_spec=pltpu.PrefetchScalarGridSpec(
            num_scalar_prefetch=1,
            grid=(steps,),
            in_specs=[whole] * 8
            + [
                pl.BlockSpec((1, D, WBLOCK), lambda f, g: (0, 0, g[0] * steps + f)),
                pl.BlockSpec((1, WBLOCK, D), lambda f, g: (0, g[0] * steps + f, 0)),
            ],
            out_specs=[
                pl.BlockSpec((1, D, WBLOCK), lambda f, g: (0, 0, f)),
                pl.BlockSpec((1, WBLOCK, D), lambda f, g: (0, f, 0)),
            ],
        ),
        out_shape=[
            jax.ShapeDtypeStruct((1, D, D), f32),
            jax.ShapeDtypeStruct((1, D, D), f32),
        ],
        compiler_params=pltpu.CompilerParams(vmem_limit_bytes=48 * 1024 * 1024),
        cost_estimate=pl.CostEstimate(
            flops=32 * SLOTS * D * D, bytes_accessed=14 * 1024 * 1024, transcendentals=0
        ),
    )(group, *rows, *grads, w_in, w_down)


def norm_backward(values, grads, gain):
    inverse = inverse_rms(values)
    normed = values * inverse
    per_gain = grads * normed
    scaled = grads * gain
    back = inverse * (scaled - normed * jnp.mean(scaled * normed, axis=-1, keepdims=True))
    return back, per_gain


def column_sums(values):
    return dot(values, jnp.ones((TOK, 128), f32), TN, HIGHEST)


def route_backward(pos, *refs):
    (routes, out_grad, attended, after, ffn_in, router, gate, placer, returned, grad_back, weights) = refs[:11]
    block_out, grad_after, grad_att, keep, send, whole = refs[11:]
    gain = dot(lane_zero(), weights[:, D + 128 : D + 256], NT)[0:1]
    grad_mix = out_grad[...].astype(f32)
    after_attn = after[...]
    gates = gate[...]
    expert_out = dot(placer[...], returned[...], NN)
    block_out[...] = (after_attn + gates * expert_out).astype(bf16)
    grad_gate = jnp.sum(grad_mix * expert_out, axis=-1, keepdims=True)
    lane = lax.broadcasted_iota(jnp.int32, (TOK, 128), 1)
    chosen = (routes[...] == lane).astype(f32)
    grad_logits = (router[...] * (chosen - gates) * grad_gate).astype(bf16)
    grad_ffn = dot(placer[...], grad_back[...], NN) + dot(grad_logits, weights[:, D : D + 128], NT)
    back, per_gain = norm_backward(after_attn, grad_ffn, gain)
    grad_after_attn = grad_mix + back
    grad_after[...] = grad_after_attn
    branch = grad_after_attn.astype(bf16)
    grad_att[...] = dot(branch, weights[:, :D], NT).astype(bf16)
    whole[:, :D] = dot(attended[...], branch, TN).astype(bf16)
    whole[:, D : D + 128] = dot(ffn_in[...], grad_logits, TN).astype(bf16)
    whole[:, D + 128 :] = column_sums(per_gain).astype(bf16)
    arrange_pieces(pos, whole, keep, send)


def attention_backward(pos, x_ref, attn_in, projected, probs, grad_att, grad_after, weights, *refs):
    grad_in, keep, send, grad_projected, diagonals, whole = refs
    left = lax.broadcasted_iota(jnp.int32, (TOK, 128), 1) < 64
    diagonals[...] = jnp.zeros_like(diagonals)

    def pair_step(pair, carry):
        start = pair * 128
        at_query = pl.ds(pl.multiple_of(start, 128), 128)
        at_key = pl.ds(pl.multiple_of(start + D, 128), 128)
        at_value = pl.ds(pl.multiple_of(start + 2 * D, 128), 128)
        queries, keys, values = projected[:, at_query], projected[:, at_key], projected[:, at_value]
        grads = grad_att[:, at_query]
        to_query, to_key, to_value = [], [], []
        for side in range(2):
            mine = left if side == 0 else jnp.logical_not(left)
            own = jnp.where(mine, grads, jnp.zeros_like(grads))
            share16 = probs[2 * pair + side]
            share = share16.astype(f32)
            grad_probs = dot(own, values, NT)
            to_value.append(dot(share16, grads, TN))
            mixed = share * grad_probs
            grad_scores = mixed - share * jnp.sum(mixed, axis=-1, keepdims=True)
            grad16 = grad_scores.astype(bf16)
            to_query.append(dot(grad16, keys, NN))
            to_key.append(dot(grad16, queries, TN))
            rounded = grad16.astype(f32)
            total = jnp.zeros((8, 512), f32)
            blank = jnp.zeros((8, 256), f32)
            for g in range(32):
                rows = jnp.concatenate([rounded[8 * g : 8 * g + 8], blank], axis=1)
                total = total + pltpu.roll(rows, 255 - 8 * g, 1)
            diagonals[2 * pair + side] = total
        grad_projected[:, at_query] = (score_scale * jnp.where(left, *to_query)).astype(bf16)
        grad_projected[:, at_key] = (score_scale * jnp.where(left, *to_key)).astype(bf16)
        grad_projected[:, at_value] = jnp.where(left, *to_value).astype(bf16)
        return carry

    lax.fori_loop(0, HEADS // 2, pair_step, 0)
    for part in range(3):
        columns = slice(part * D, (part + 1) * D)
        whole[:, columns] = dot(attn_in[...], grad_projected[:, columns], TN).astype(bf16)
    grad_attn_input = dot(grad_projected[...], weights[:, :QKV], NT)
    gain = dot(lane_zero(), weights[:, QKV : QKV + 128], NT)[0:1]
    x = x_ref[...].astype(f32)
    back, per_gain = norm_backward(x, grad_attn_input, gain)
    grad_in[...] = grad_after[...] + back
    whole[:, QKV : QKV + 128] = column_sums(per_gain).astype(bf16)
    buckets = diagonal_buckets()
    per_bucket = jnp.zeros((BUCKETS, 128), f32)
    for row in range(8):
        per_bucket = per_bucket + dot(bucket_hot(buckets, row), diagonals[:, row, :], NT, HIGHEST)
    whole[:, QKV + 128 :] = dot(owner_rows(), per_bucket.astype(bf16), TN).astype(bf16)
    arrange_pieces(pos, whole, keep, send)


def on_device(
    hidden_in,
    doc_ids,
    routes,
    attn_gain,
    w_query,
    w_key,
    w_value,
    w_out,
    rel_bias,
    ffn_gain,
    w_router,
    w_in,
    w_down,
    out_grad,
):
    place = lax.axis_index("exp")
    core = place % 2
    pos = jnp.stack([place // 8, (place // 2) % 4, core]).astype(jnp.int32)
    group = lax.axis_index("rep").astype(jnp.int32).reshape(1)

    def padded(value):
        return jnp.pad(value, ((0, 24 - value.shape[0]), (0, 128 - value.shape[1])))

    shard1 = jnp.concatenate(
        [w_query, w_key, w_value, padded(attn_gain[:, None]), padded(rel_bias)], axis=1
    )
    shard2 = jnp.concatenate([w_out, padded(w_router), padded(ffn_gain[:, None])], axis=1)
    pieces1 = gather_pieces(shard1, core)
    pieces2 = gather_pieces(shard2, core)
    doc_col = doc_ids.reshape(TOK, 1)
    doc_row = doc_ids.reshape(1, TOK)

    weights1, attn_in, projected, probs, attended = call(
        attention_forward,
        [
            ((D, WIDE1), bf16),
            ((TOK, D), bf16),
            ((TOK, QKV), bf16),
            ((HEADS, TOK, TOK), bf16),
            ((TOK, D), bf16),
        ],
        pos,
        hidden_in,
        doc_col,
        doc_row,
        *pieces1,
        scratch=[pltpu.VMEM((16, 8, 512), f32)],
        flops=8_000_000_000,
        bytes_accessed=14_000_000,
    )
    weights2, after, ffn_in, router, gate, placer, outbound, grad_outbound = call(
        route_forward,
        [
            ((D, WIDE2), bf16),
            ((TOK, D), f32),
            ((TOK, D), bf16),
            ((TOK, 128), f32),
            ((TOK, 1), f32),
            ((TOK, SLOTS), bf16),
            ((SLOTS, D), bf16),
            ((SLOTS, D), bf16),
        ],
        pos,
        hidden_in,
        routes,
        out_grad,
        attended,
        *pieces2,
        flops=4_000_000_000,
        bytes_accessed=8_000_000,
    )

    def exchange(value):
        return lax.all_to_all(
            value.reshape(EXPERTS, CAP, D), "exp", split_axis=0, concat_axis=0, tiled=True
        ).reshape(SLOTS, D)

    slot_rows = exchange(outbound)
    slot_grads = exchange(grad_outbound)
    all_rows = [slot_rows] + [lax.ppermute(slot_rows, "rep", z_shift(k)) for k in (1, 2, 3)]
    all_grads = [slot_grads] + [lax.ppermute(slot_grads, "rep", z_shift(k)) for k in (1, 2, 3)]
    produced, slope = run_expert_forward(slot_rows, w_in, w_down)
    returned = exchange(produced)
    grad_rows = run_expert_backward(slot_grads, slope, w_in, w_down)
    grad_back = exchange(grad_rows)
    grad_w_in, grad_w_down = run_expert_weights(group, all_rows, all_grads, w_in, w_down)

    quarter2, quarter1 = WIDE2 // 4, WIDE1 // 4
    block_out, grad_after, grad_att, keep2, send2 = call(
        route_backward,
        [
            ((TOK, D), bf16),
            ((TOK, D), f32),
            ((TOK, D), bf16),
            ((8, 4, 48, quarter2), bf16),
            ((8, 4, 48, quarter2), bf16),
        ],
        pos,
        routes,
        out_grad,
        attended,
        after,
        ffn_in,
        router,
        gate,
        placer,
        returned,
        grad_back,
        weights2,
        scratch=[pltpu.VMEM((D, WIDE2), bf16)],
        flops=4_000_000_000,
        bytes_accessed=10_000_000,
    )
    reduced2 = reduce_pieces(pos, core, keep2, send2)
    grad_in, keep1, send1 = call(
        attention_backward,
        [
            ((TOK, D), f32),
            ((8, 4, 48, quarter1), bf16),
            ((8, 4, 48, quarter1), bf16),
        ],
        pos,
        hidden_in,
        attn_in,
        projected,
        probs,
        grad_att,
        grad_after,
        weights1,
        scratch=[
            pltpu.VMEM((TOK, QKV), bf16),
            pltpu.VMEM((128, 8, 512), f32),
            pltpu.VMEM((D, WIDE1), bf16),
        ],
        flops=16_000_000_000,
        bytes_accessed=14_000_000,
    )
    reduced1 = reduce_pieces(pos, core, keep1, send1)
    return (
        block_out,
        grad_in,
        reduced1[:, QKV],
        reduced1[:, :D],
        reduced1[:, D : 2 * D],
        reduced1[:, 2 * D : QKV],
        reduced2[:, :D],
        reduced1[0:1, QKV + 128 : QKV + 128 + HEADS],
        reduced2[:, D + 128],
        reduced2[:, D : D + EXPERTS],
        grad_w_in,
        grad_w_down,
    )


def solution(mesh):
    in_specs = (
        P(("rep", "exp"), None),
        P(("rep", "exp")),
        P(("rep", "exp"), None),
        P("exp"),
        P("exp", None),
        P("exp", None),
        P("exp", None),
        P("exp", None),
        P("exp", None),
        P("exp"),
        P("exp", None),
        P("exp", None, None),
        P("exp", None, None),
        P(("rep", "exp"), None),
    )
    out_specs = (
        P(("rep", "exp"), None),
        P(("rep", "exp"), None),
        P("exp"),
        P("exp", None),
        P("exp", None),
        P("exp", None),
        P("exp", None),
        P("exp", None),
        P("exp"),
        P("exp", None),
        P("exp", None, "rep"),
        P("exp", "rep", None),
    )
    return jax.shard_map(
        on_device, mesh=mesh, in_specs=in_specs, out_specs=out_specs, check_vma=False
    )
```

```python
import jax
import jax.numpy as jnp
from jax import lax
from jax.experimental import pallas as pl
from jax.experimental.pallas import tpu as pltpu
from jax.sharding import PartitionSpec as P

HEADS = 12
HEAD_DIM = 64
BUCKETS = 32
D = 768
FF = 3072
TOK = 256
EXPERTS = 32
CAP = 16
SLOTS = EXPERTS * CAP
HALF = D // 2
QKV = 3 * HALF
WIDE1 = QKV + 128
WIDE2 = D + 128
WIDE = D + 128
SENT = QKV + HALF + 128
AT_FFN = EXPERTS
AT_ATTN = EXPERTS + 1
AT_BIAS = EXPERTS + 2

eps = 1e-06
reach_marks = (12, 16, 23, 32, 46, 64, 91)
big_negative = -1000000000.0
score_scale = HEAD_DIM ** (-0.5)

f32 = jnp.float32
bf16 = jnp.bfloat16
HIGHEST = lax.Precision.HIGHEST

NN = ((1,), (0,))
NT = ((1,), (1,))
TN = ((0,), (0,))

SWAP = [(i, i ^ 1) for i in range(32)]


def z_shift(step):
    return [(i, (i + step) % 4) for i in range(4)]


def on_exp(value, pairs):
    return lax.ppermute(value, "exp", pairs)


def dot(left, right, dims, precision=None):
    return lax.dot_general(
        left, right, (dims, ((), ())), precision=precision, preferred_element_type=f32
    )


def call(body, outs, *args, scratch=(), smem=1, after=(), flops=0, bytes_accessed=0):
    count = len(args)
    specs = [
        pl.BlockSpec(memory_space=pltpu.SMEM) if i < smem else pl.BlockSpec()
        for i in range(count)
    ]
    specs += [pl.BlockSpec(memory_space=pl.ANY) for _ in after]

    def run(*refs):
        body(*refs[:count], *refs[count + len(after) :])

    return pl.pallas_call(
        run,
        out_shape=[jax.ShapeDtypeStruct(shape, kind) for shape, kind in outs],
        in_specs=specs,
        out_specs=[pl.BlockSpec() for _ in outs],
        scratch_shapes=list(scratch),
        compiler_params=pltpu.CompilerParams(vmem_limit_bytes=60 * 1024 * 1024),
        cost_estimate=pl.CostEstimate(
            flops=flops, bytes_accessed=bytes_accessed, transcendentals=0
        ),
    )(*args, *after)


def pack_weights(query, key, value, out, router, attn_gain, ffn_gain, bias, packed, beside):
    same = lax.broadcasted_iota(jnp.int32, (24, 24), 0) == lax.broadcasted_iota(
        jnp.int32, (24, 24), 1
    )

    def column(row):
        spread = jnp.broadcast_to(row[...].astype(f32), (24, 24))
        return jnp.sum(jnp.where(same, spread, 0.0), axis=1, keepdims=True)

    first = lax.broadcasted_iota(jnp.int32, (24, HEADS), 0) == 0
    table = jnp.where(first, jnp.broadcast_to(bias[...].astype(f32), (24, HEADS)), 0.0)
    extra = jnp.concatenate(
        [
            router[...].astype(f32),
            column(ffn_gain),
            column(attn_gain),
            table,
            jnp.zeros((24, 128 - AT_BIAS - HEADS), f32),
        ],
        axis=1,
    ).astype(bf16)
    beside[:, :D] = out[...]
    beside[:, D:] = extra
    for core in range(2):
        columns = slice(core * HALF, (core + 1) * HALF)
        half = jnp.concatenate(
            [query[:, columns], key[:, columns], value[:, columns], extra], axis=1
        )
        for chip in range(16):
            packed[2 * chip + core] = half


def sum_parts(parts, own):
    for core in range(2):
        total = parts[core].astype(f32)
        for chip in range(1, 16):
            total = total + parts[2 * chip + core].astype(f32)
        own[:, core * SENT : (core + 1) * SENT] = total.astype(bf16)


def diagonal_buckets():
    lane = lax.broadcasted_iota(jnp.int32, (8, 512), 1)
    row = lax.broadcasted_iota(jnp.int32, (8, 512), 0)
    relative = lane - row - 255
    distance = jnp.abs(relative)
    far = jnp.full((8, 512), 8, jnp.int32)
    for mark in reach_marks:
        far = far + (distance >= mark).astype(jnp.int32)
    return jnp.where(distance < 8, distance, far) + jnp.where(relative > 0, 16, 0)


def bucket_hot(buckets, row):
    which = lax.broadcasted_iota(jnp.int32, (BUCKETS, 512), 0)
    return (which == jnp.broadcast_to(buckets[row : row + 1], (BUCKETS, 512))).astype(f32)


def owner_rows():
    row = lax.broadcasted_iota(jnp.int32, (BUCKETS, D), 0)
    column = lax.broadcasted_iota(jnp.int32, (BUCKETS, D), 1)
    return (column == row * 24).astype(bf16)


def gain_row(extra, lane):
    pick = (lax.broadcasted_iota(jnp.int32, (8, 128), 1) == lane).astype(bf16)
    return dot(pick, extra, NT)[0:1]


def inverse_rms(values):
    return lax.rsqrt(jnp.mean(values * values, axis=-1, keepdims=True) + eps)


def attention_forward(pos, x_own, x_other, doc_col, doc_row, weights, *refs):
    attn_in, projected, probs, attended_own, attended_other, base = refs
    extra = weights[:, QKV:]
    gain = gain_row(extra, AT_ATTN)
    head = lax.broadcasted_iota(jnp.int32, (128, 16), 1)
    moved = (lax.broadcasted_iota(jnp.int32, (128, 16), 0) == head + AT_BIAS).astype(bf16)
    table = dot(dot(extra, moved, NN).astype(bf16), owner_rows(), ((0,), (1,)))
    buckets = diagonal_buckets()
    for row in range(8):
        base[:, row, :] = dot(table.astype(bf16), bucket_hot(buckets, row).astype(bf16), NN)
    for block, x_ref in enumerate((x_own, x_other)):
        x = x_ref[...].astype(f32)
        attn_in[block * TOK : (block + 1) * TOK] = (x * inverse_rms(x) * gain).astype(bf16)
    for part in range(3):
        columns = slice(part * HALF, (part + 1) * HALF)
        projected[:, columns] = dot(attn_in[...], weights[:, columns], NN).astype(bf16)
    left = lax.broadcasted_iota(jnp.int32, (TOK, 128), 1) < 64
    first_head = pos[2] * (HEADS // 2)
    for block, attended in enumerate((attended_own, attended_other)):
        rows = slice(block * TOK, (block + 1) * TOK)
        same = doc_col[rows] == doc_row[block : block + 1]

        def pair_step(pair, carry):
            start = pair * 128
            queries = projected[rows, pl.ds(pl.multiple_of(start, 128), 128)]
            keys = projected[rows, pl.ds(pl.multiple_of(start + HALF, 128), 128)]
            values = projected[rows, pl.ds(pl.multiple_of(start + 2 * HALF, 128), 128)]
            results = []
            for side in range(2):
                mine = left if side == 0 else jnp.logical_not(left)
                own = jnp.where(mine, queries, jnp.zeros_like(queries))
                diagonal = base[first_head + 2 * pair + side]
                bias = jnp.concatenate(
                    [pltpu.roll(diagonal, 257 + 8 * g, 1)[:, :256] for g in range(32)], axis=0
                )
                scores = jnp.where(same, score_scale * dot(own, keys, NT) + bias, big_negative)
                top = jnp.max(scores, axis=-1, keepdims=True)
                grown = jnp.exp(scores - top)
                share = grown * (1.0 / jnp.sum(grown, axis=-1, keepdims=True))
                share = share.astype(bf16)
                probs[block * (HEADS // 2) + 2 * pair + side] = share
                results.append(dot(share, values, NN))
            attended[:, pl.ds(pl.multiple_of(start, 128), 128)] = jnp.where(
                left, results[0], results[1]
            ).astype(bf16)
            return carry

        lax.fori_loop(0, HEADS // 4, pair_step, 0)


def in_parts(value, rows):
    lane = lax.broadcasted_iota(jnp.int32, (rows, 128), 1)
    high = value.astype(bf16).astype(f32)
    middle = (value - high).astype(bf16).astype(f32)
    low = value - high - middle
    parts = jnp.where(lane == 0, high, jnp.where(lane == 1, middle, jnp.where(lane == 2, low, 0.0)))
    return parts.astype(bf16)


def from_parts(parts):
    return jnp.sum(parts.astype(f32), axis=-1, keepdims=True)


def place_grads(routes, out_grad, placer, placed_grads):
    lane = lax.broadcasted_iota(jnp.int32, (TOK, 128), 1)
    chosen = routes[...] == lane
    earlier = (
        lax.broadcasted_iota(jnp.int32, (TOK, TOK), 1)
        < lax.broadcasted_iota(jnp.int32, (TOK, TOK), 0)
    ).astype(bf16)
    counts = dot(earlier, chosen.astype(bf16), NN)
    rank = jnp.sum(jnp.where(chosen, counts, 0.0), axis=-1, keepdims=True)
    slot = routes[...] * CAP + rank.astype(jnp.int32)
    placed = (slot == lax.broadcasted_iota(jnp.int32, (TOK, SLOTS), 1)).astype(bf16)
    placer[...] = placed
    placed_grads[...] = dot(placed, out_grad[...], TN).astype(bf16)


def hold(value, until, out):
    del value, until, out


def hold_until(value, until):
    return pl.pallas_call(
        hold,
        out_shape=jax.ShapeDtypeStruct(value.shape, value.dtype),
        in_specs=[pl.BlockSpec(memory_space=pl.ANY)] * 2,
        out_specs=pl.BlockSpec(memory_space=pl.ANY),
        input_output_aliases={0: 0},
    )(value, until)


def core_halves(pos):
    own = pl.ds(pl.multiple_of(pos[2] * HALF, 128), HALF)
    other = pl.ds(pl.multiple_of((1 - pos[2]) * HALF, 128), HALF)
    return own, other


def route_forward(pos, x_ref, routes, att_own, att_other, placer, weights, *refs):
    after, ffn_in, router, gate, outbound = refs
    own, other = core_halves(pos)
    extra = weights[:, D:]
    gain = gain_row(extra, AT_FFN)
    after_attn = (
        x_ref[...].astype(f32)
        + dot(att_own[...], weights[own, :D], NN)
        + dot(att_other[...], weights[other, :D], NN)
    )
    after[...] = after_attn
    ffn_input = (after_attn * inverse_rms(after_attn) * gain).astype(bf16)
    ffn_in[...] = ffn_input
    lane = lax.broadcasted_iota(jnp.int32, (TOK, 128), 1)
    logits = dot(ffn_input, extra, NN)
    logits = jnp.where(lane < EXPERTS, logits, -1e30)
    grown = jnp.exp(logits - jnp.max(logits, axis=-1, keepdims=True))
    share = grown / jnp.sum(grown, axis=-1, keepdims=True)
    router[...] = share
    gates = jnp.sum(jnp.where(routes[...] == lane, share, 0.0), axis=-1, keepdims=True)
    gate[...] = gates
    outbound[:, :D] = dot(placer[...], ffn_input, TN).astype(bf16)
    outbound[:, D:] = dot(placer[...], in_parts(gates, TOK), TN).astype(bf16)


def gelu_parts(pre):
    square = pre * pre
    inner = 0.7978845608028654 * pre * (1.0 + 0.044715 * square)
    bend = jnp.tanh(inner)
    cdf = 0.5 * (1.0 + bend)
    slope = cdf + 0.5 * pre * (1.0 - bend * bend) * (
        0.7978845608028654 * (1.0 + 0.134145 * square)
    )
    return pre * cdf, slope


def expert_block(rows, mix, w_in, w_down, produced, back, total, back_total, grads):
    step = pl.program_id(0)

    @pl.when(step == 0)
    def _():
        grads[...] = (from_parts(rows[:, D:]) * mix[...].astype(f32)).astype(bf16)

    active, slope = gelu_parts(dot(rows[:, :D], w_in[0], NN))
    grad_pre = (dot(grads[...], w_down[0], NT) * slope).astype(bf16)
    forward = dot(active.astype(bf16), w_down[0], NN)
    backward = dot(grad_pre, w_in[0], NT)

    @pl.when(step == 0)
    def _():
        total[...] = forward
        back_total[...] = backward

    @pl.when(step > 0)
    def _():
        total[...] += forward
        back_total[...] += backward

    @pl.when(step == pl.num_programs(0) - 1)
    def _():
        out = total[...].astype(bf16)
        produced[...] = out
        back[:, :D] = back_total[...].astype(bf16)
        per_gate = jnp.sum(mix[...].astype(f32) * out.astype(f32), axis=-1, keepdims=True)
        back[:, D:] = in_parts(per_gate, SLOTS)


def expert_weights(pos, *refs):
    all_rows, all_mix, w_in, w_down, _, grad_in, grad_down = refs
    for k in range(4):
        group = slice(k * SLOTS, (k + 1) * SLOTS)
        own = all_rows[group, :D]
        grads = (from_parts(all_rows[group, D:]) * all_mix[group].astype(f32)).astype(bf16)
        active, slope = gelu_parts(dot(own, w_in[0], NN))
        grad_pre = (dot(grads, w_down[0], NT) * slope).astype(bf16)
        to_in = dot(own, grad_pre, TN)
        to_down = dot(active.astype(bf16), grads, TN)
        if k == 0:
            grad_in[0] = to_in
            grad_down[0] = to_down
        else:
            grad_in[0] += to_in
            grad_down[0] += to_down


BLOCK = 512
WBLOCK = 256


def run_expert(rows, mix, w_in, w_down):
    wide = pl.BlockSpec((SLOTS, WIDE), lambda f: (0, 0))
    whole = pl.BlockSpec((SLOTS, D), lambda f: (0, 0))
    return pl.pallas_call(
        expert_block,
        grid=(FF // BLOCK,),
        in_specs=[
            wide,
            whole,
            pl.BlockSpec((1, D, BLOCK), lambda f: (0, 0, f)),
            pl.BlockSpec((1, BLOCK, D), lambda f: (0, f, 0)),
        ],
        out_specs=[whole, wide],
        out_shape=[
            jax.ShapeDtypeStruct((SLOTS, D), bf16),
            jax.ShapeDtypeStruct((SLOTS, WIDE), bf16),
        ],
        scratch_shapes=[
            pltpu.VMEM((SLOTS, D), f32),
            pltpu.VMEM((SLOTS, D), f32),
            pltpu.VMEM((SLOTS, D), bf16),
        ],
        compiler_params=pltpu.CompilerParams(vmem_limit_bytes=60 * 1024 * 1024),
        cost_estimate=pl.CostEstimate(
            flops=8 * SLOTS * D * FF, bytes_accessed=14 * 1024 * 1024, transcendentals=0
        ),
    )(rows, mix, w_in, w_down)


def run_expert_weights(group, rows, mix, w_in, w_down, after):
    steps = D // WBLOCK
    return pl.pallas_call(
        expert_weights,
        grid_spec=pltpu.PrefetchScalarGridSpec(
            num_scalar_prefetch=1,
            grid=(steps,),
            in_specs=[
                pl.BlockSpec((4 * SLOTS, WIDE), lambda f, g: (0, 0)),
                pl.BlockSpec((4 * SLOTS, D), lambda f, g: (0, 0)),
                pl.BlockSpec((1, D, WBLOCK), lambda f, g: (0, 0, g[0] * steps + f)),
                pl.BlockSpec((1, WBLOCK, D), lambda f, g: (0, g[0] * steps + f, 0)),
                pl.BlockSpec(memory_space=pl.ANY),
            ],
            out_specs=[
                pl.BlockSpec((1, D, WBLOCK), lambda f, g: (0, 0, f)),
                pl.BlockSpec((1, WBLOCK, D), lambda f, g: (0, f, 0)),
            ],
        ),
        out_shape=[
            jax.ShapeDtypeStruct((1, D, D), f32),
            jax.ShapeDtypeStruct((1, D, D), f32),
        ],
        compiler_params=pltpu.CompilerParams(vmem_limit_bytes=60 * 1024 * 1024),
        cost_estimate=pl.CostEstimate(
            flops=32 * SLOTS * D * D, bytes_accessed=14 * 1024 * 1024, transcendentals=0
        ),
    )(group, rows, mix, w_in, w_down, after)


def mix_out(after, gate, placer, returned, block_out):
    expert_out = dot(placer[...], returned[...], NN)
    block_out[...] = (after[...] + gate[...] * expert_out).astype(bf16)


def norm_backward(values, grads, gain):
    inverse = inverse_rms(values)
    normed = values * inverse
    per_gain = grads * normed
    scaled = grads * gain
    back = inverse * (scaled - normed * jnp.mean(scaled * normed, axis=-1, keepdims=True))
    return back, per_gain


def column_sums(values):
    return dot(values, jnp.ones((values.shape[0], 128), f32), TN, HIGHEST)


def route_backward(pos, *refs):
    (routes, out_grad, att_own, att_other, after, ffn_in, router, gate, placer, grad_back, weights) = refs[:11]
    grad_after, grad_own, grad_other, keep, send, whole = refs[11:]
    extra_weights = weights[:, D:]
    gain = gain_row(extra_weights, AT_FFN)
    grad_mix = out_grad[...].astype(f32)
    after_attn = after[...]
    gates = gate[...]
    lane = lax.broadcasted_iota(jnp.int32, (TOK, 128), 1)
    grad_gate = from_parts(dot(placer[...], grad_back[:, D:], NN))
    chosen = (routes[...] == lane).astype(f32)
    grad_logits = (router[...] * (chosen - gates) * grad_gate).astype(bf16)
    router_weights = jnp.where(
        lax.broadcasted_iota(jnp.int32, (D, 128), 1) < EXPERTS, extra_weights, jnp.zeros((D, 128), bf16)
    )
    grad_ffn = dot(placer[...], grad_back[:, :D], NN) + dot(grad_logits, router_weights, NT)
    back, per_gain = norm_backward(after_attn, grad_ffn, gain)
    grad_after_attn = grad_mix + back
    grad_after[...] = grad_after_attn
    branch = grad_after_attn.astype(bf16)
    own, other = core_halves(pos)
    grad_own[...] = dot(branch, weights[own, :D], NT).astype(bf16)
    grad_other[...] = dot(branch, weights[other, :D], NT).astype(bf16)
    whole[own, :] = dot(att_own[...], branch, TN).astype(bf16)
    whole[other, :] = dot(att_other[...], branch, TN).astype(bf16)
    keep[:, :HALF] = whole[:, own]
    send[...] = whole[:, other]
    tall = lax.broadcasted_iota(jnp.int32, (D, 128), 1)
    extra = dot(ffn_in[...], grad_logits, TN)
    keep[:, HALF:] = jnp.where(tall == AT_FFN, column_sums(per_gain), extra).astype(bf16)


def attention_backward(pos, projected, probs, grad_own, grad_other, grad_projected, diagonals):
    left = lax.broadcasted_iota(jnp.int32, (TOK, 128), 1) < 64
    diagonals[...] = jnp.zeros_like(diagonals)
    first_head = pos[2] * (HEADS // 2)
    for block, grad_att in enumerate((grad_own, grad_other)):
        rows = slice(block * TOK, (block + 1) * TOK)

        def pair_step(pair, carry):
            start = pair * 128
            at_query = pl.ds(pl.multiple_of(start, 128), 128)
            at_key = pl.ds(pl.multiple_of(start + HALF, 128), 128)
            at_value = pl.ds(pl.multiple_of(start + 2 * HALF, 128), 128)
            queries, keys, values = (
                projected[rows, at_query],
                projected[rows, at_key],
                projected[rows, at_value],
            )
            grads = grad_att[:, at_query]
            to_query, to_key, to_value = [], [], []
            for side in range(2):
                mine = left if side == 0 else jnp.logical_not(left)
                own = jnp.where(mine, grads, jnp.zeros_like(grads))
                share16 = probs[block * (HEADS // 2) + 2 * pair + side]
                share = share16.astype(f32)
                grad_probs = dot(own, values, NT)
                to_value.append(dot(share16, grads, TN))
                mixed = share * grad_probs
                grad_scores = mixed - share * jnp.sum(mixed, axis=-1, keepdims=True)
                grad16 = grad_scores.astype(bf16)
                to_query.append(dot(grad16, keys, NN))
                to_key.append(dot(grad16, queries, TN))
                rounded = grad16.astype(f32)
                total = jnp.zeros((8, 512), f32)
                blank = jnp.zeros((8, 256), f32)
                for g in range(32):
                    lines = jnp.concatenate([rounded[8 * g : 8 * g + 8], blank], axis=1)
                    total = total + pltpu.roll(lines, 255 - 8 * g, 1)
                diagonals[first_head + 2 * pair + side] += total
            grad_projected[rows, at_query] = (score_scale * jnp.where(left, *to_query)).astype(bf16)
            grad_projected[rows, at_key] = (score_scale * jnp.where(left, *to_key)).astype(bf16)
            grad_projected[rows, at_value] = jnp.where(left, *to_value).astype(bf16)
            return carry

        lax.fori_loop(0, HEADS // 4, pair_step, 0)


def weights_backward(x_own, x_other, attn_in, grad_projected, weights, diagonals, keep, got, *refs):
    whole, to_own, to_other = refs
    whole[:, :QKV] = dot(attn_in[...], grad_projected[...], TN).astype(bf16)
    whole[:, QKV : QKV + HALF] = (keep[:, :HALF].astype(f32) + got[...].astype(f32)).astype(bf16)
    sums = jnp.zeros((D, 128), f32)
    for block, (x_ref, out) in enumerate(((x_own, to_own), (x_other, to_other))):
        rows = slice(block * TOK, (block + 1) * TOK)
        grads = dot(grad_projected[rows], weights[:, :QKV], NT)
        out[...] = grads
        x = x_ref[...].astype(f32)
        sums = sums + column_sums(grads * (x * inverse_rms(x)))
    buckets = diagonal_buckets()
    per_bucket = jnp.zeros((BUCKETS, 16), f32)
    for row in range(8):
        per_bucket = per_bucket + dot(bucket_hot(buckets, row), diagonals[:, row, :], NT, HIGHEST)
    head = lax.broadcasted_iota(jnp.int32, (16, 128), 0)
    moved = (lax.broadcasted_iota(jnp.int32, (16, 128), 1) == head + AT_BIAS).astype(bf16)
    per_bucket = dot(per_bucket.astype(bf16), moved, NN)
    tall = lax.broadcasted_iota(jnp.int32, (D, 128), 1)
    extra = keep[:, HALF:].astype(f32) + dot(owner_rows(), per_bucket.astype(bf16), TN)
    whole[:, QKV + HALF :] = jnp.where(tall == AT_ATTN, sums, extra).astype(bf16)


def input_backward(x_ref, grad_after, to_own, got, weights, grad_in):
    gain = gain_row(weights[:, QKV:], AT_ATTN)
    back, _ = norm_backward(x_ref[...].astype(f32), to_own[...] + got[...], gain)
    grad_in[...] = grad_after[...] + back


def sum_groups(own, one, two, three, query, key, value, out, router, attn_gain, ffn_gain, bias):
    total = (own[...].astype(f32) + two[...].astype(f32)) + (
        one[...].astype(f32) + three[...].astype(f32)
    )
    for part, target in enumerate((query, key, value, out)):
        target[:, :HALF] = total[:, part * HALF : (part + 1) * HALF]
        target[:, HALF:] = total[:, SENT + part * HALF : SENT + (part + 1) * HALF]
    extra = total[:, SENT - 128 : SENT] + total[:, 2 * SENT - 128 :]
    same = lax.broadcasted_iota(jnp.int32, (24, 24), 0) == lax.broadcasted_iota(
        jnp.int32, (24, 24), 1
    )

    def row(lane):
        spread = jnp.broadcast_to(extra[:, lane : lane + 1], (24, 24))
        return jnp.sum(jnp.where(same, spread, 0.0), axis=0, keepdims=True)

    router[...] = extra[:, :EXPERTS]
    attn_gain[...] = row(AT_ATTN)
    ffn_gain[...] = row(AT_FFN)
    bias[...] = extra[0:1, AT_BIAS : AT_BIAS + HEADS]


def on_device(
    hidden_in,
    doc_ids,
    routes,
    attn_gain,
    w_query,
    w_key,
    w_value,
    w_out,
    rel_bias,
    ffn_gain,
    w_router,
    w_in,
    w_down,
    out_grad,
):
    place = lax.axis_index("exp").astype(jnp.int32)
    pos = jnp.stack([place // 8, (place // 2) % 4, place % 2])
    group = lax.axis_index("rep").astype(jnp.int32).reshape(1)

    def over_exp(value):
        return lax.all_to_all(value, "exp", split_axis=0, concat_axis=0, tiled=True)

    def over_groups(value):
        return lax.all_gather(value, "rep", axis=0, tiled=True)

    packed, beside = call(
        pack_weights,
        [((EXPERTS, 24, WIDE1), bf16), ((24, WIDE2), bf16)],
        w_query,
        w_key,
        w_value,
        w_out,
        w_router,
        attn_gain.reshape(1, 24),
        ffn_gain.reshape(1, 24),
        rel_bias,
        smem=0,
    )
    weights2 = lax.all_gather(beside, "exp", axis=0, tiled=True)
    weights1 = over_exp(packed).reshape(D, WIDE1)
    x_other = on_exp(hidden_in, SWAP)
    doc_row = jnp.stack([doc_ids, on_exp(doc_ids, SWAP)])
    doc_col = doc_row.reshape(2 * TOK, 1)

    placer, placed_grads = call(
        place_grads,
        [((TOK, SLOTS), bf16), ((SLOTS, D), bf16)],
        routes,
        out_grad,
        smem=0,
        flops=500_000_000,
        bytes_accessed=2_000_000,
    )

    def exchange(value):
        width = value.shape[1]
        return over_exp(value.reshape(EXPERTS, CAP, width)).reshape(SLOTS, width)

    slot_mix = exchange(hold_until(placed_grads, weights1))

    attn_in, projected, probs, att_own, att_send = call(
        attention_forward,
        [
            ((2 * TOK, D), bf16),
            ((2 * TOK, QKV), bf16),
            ((HEADS, TOK, TOK), bf16),
            ((TOK, HALF), bf16),
            ((TOK, HALF), bf16),
        ],
        pos,
        hidden_in,
        x_other,
        doc_col,
        doc_row,
        weights1,
        scratch=[pltpu.VMEM((16, 8, 512), f32)],
        flops=9_000_000_000,
        bytes_accessed=10_000_000,
    )
    att_other = on_exp(att_send, SWAP)
    after, ffn_in, router, gate, outbound = call(
        route_forward,
        [
            ((TOK, D), f32),
            ((TOK, D), bf16),
            ((TOK, 128), f32),
            ((TOK, 1), f32),
            ((SLOTS, WIDE), bf16),
        ],
        pos,
        hidden_in,
        routes,
        att_own,
        att_other,
        placer,
        weights2,
        flops=3_000_000_000,
        bytes_accessed=8_000_000,
    )
    slot_rows = exchange(outbound)
    all_mix = over_groups(hold_until(slot_mix, att_send))
    all_rows = over_groups(slot_rows)
    produced, back = run_expert(slot_rows, slot_mix, w_in, w_down)
    grad_back = exchange(back)
    returned = exchange(produced)

    grad_after, grad_own, grad_send, keep, send = call(
        route_backward,
        [
            ((TOK, D), f32),
            ((TOK, HALF), bf16),
            ((TOK, HALF), bf16),
            ((D, HALF + 128), bf16),
            ((D, HALF), bf16),
        ],
        pos,
        routes,
        out_grad,
        att_own,
        att_other,
        after,
        ffn_in,
        router,
        gate,
        placer,
        grad_back,
        weights2,
        scratch=[pltpu.VMEM((D, D), bf16)],
        flops=4_000_000_000,
        bytes_accessed=10_000_000,
    )
    grad_other = on_exp(grad_send, SWAP)
    got = on_exp(send, SWAP)
    grad_projected, diagonals = call(
        attention_backward,
        [((2 * TOK, QKV), bf16), ((16, 8, 512), f32)],
        pos,
        projected,
        probs,
        grad_own,
        grad_other,
        flops=9_000_000_000,
        bytes_accessed=8_000_000,
    )
    (block_out,) = call(
        mix_out,
        [((TOK, D), bf16)],
        after,
        gate,
        placer,
        returned,
        smem=0,
        flops=200_000_000,
        bytes_accessed=3_000_000,
    )
    whole, to_own, to_send = call(
        weights_backward,
        [((D, SENT), bf16), ((TOK, D), f32), ((TOK, D), f32)],
        hidden_in,
        x_other,
        attn_in,
        grad_projected,
        weights1,
        diagonals,
        keep,
        got,
        smem=0,
        after=[block_out],
        flops=5_000_000_000,
        bytes_accessed=10_000_000,
    )
    parts = over_exp(whole.reshape(EXPERTS, 24, SENT))
    to_got = on_exp(to_send, SWAP)
    grad_w_in, grad_w_down = run_expert_weights(group, all_rows, all_mix, w_in, w_down, to_send)
    (grad_in,) = call(
        input_backward,
        [((TOK, D), f32)],
        hidden_in,
        grad_after,
        to_own,
        to_got,
        weights1,
        smem=0,
        flops=10_000_000,
        bytes_accessed=5_000_000,
    )
    (own,) = call(
        sum_parts, [((24, 2 * SENT), bf16)], parts, smem=0, after=[grad_w_in, grad_in]
    )
    others = [lax.ppermute(own, "rep", z_shift(k)) for k in (1, 2, 3)]
    (
        grad_query,
        grad_key,
        grad_value,
        grad_out,
        grad_router,
        grad_attn_gain,
        grad_ffn_gain,
        grad_rel_bias,
    ) = call(
        sum_groups,
        [((24, D), f32)] * 4
        + [((24, EXPERTS), f32), ((1, 24), f32), ((1, 24), f32), ((1, HEADS), f32)],
        own,
        *others,
        smem=0,
    )
    return (
        block_out,
        grad_in,
        grad_attn_gain.reshape(24),
        grad_query,
        grad_key,
        grad_value,
        grad_out,
        grad_rel_bias,
        grad_ffn_gain.reshape(24),
        grad_router,
        grad_w_in,
        grad_w_down,
    )


def solution(mesh):
    in_specs = (
        P(("rep", "exp"), None),
        P(("rep", "exp")),
        P(("rep", "exp"), None),
        P("exp"),
        P("exp", None),
        P("exp", None),
        P("exp", None),
        P("exp", None),
        P("exp", None),
        P("exp"),
        P("exp", None),
        P("exp", None, None),
        P("exp", None, None),
        P(("rep", "exp"), None),
    )
    out_specs = (
        P(("rep", "exp"), None),
        P(("rep", "exp"), None),
        P("exp"),
        P("exp", None),
        P("exp", None),
        P("exp", None),
        P("exp", None),
        P("exp", None),
        P("exp"),
        P("exp", None),
        P("exp", None, "rep"),
        P("exp", "rep", None),
    )
    return jax.shard_map(
        on_device, mesh=mesh, in_specs=in_specs, out_specs=out_specs, check_vma=False
    )
```

```python
import jax
import jax.numpy as jnp
from jax import lax
from jax.experimental import pallas as pl
from jax.experimental.pallas import tpu as pltpu
from jax.sharding import PartitionSpec as P

HEADS = 12
HEAD_DIM = 64
BUCKETS = 32
D = 768
FF = 3072
TOK = 256
EXPERTS = 32
CAP = 16
SLOTS = EXPERTS * CAP
HALF = D // 2
QKV = 3 * HALF
WIDE = D + 128
SENT = QKV + HALF + 128
AT_FFN = EXPERTS
AT_ATTN = EXPERTS + 1
AT_BIAS = EXPERTS + 2

eps = 1e-06
reach_marks = (12, 16, 23, 32, 46, 64, 91)
big_negative = -1000000000.0
score_scale = HEAD_DIM ** (-0.5)

f32 = jnp.float32
bf16 = jnp.bfloat16
HIGHEST = lax.Precision.HIGHEST

NN = ((1,), (0,))
NT = ((1,), (1,))
TN = ((0,), (0,))

SWAP = [(i, i ^ 1) for i in range(32)]


def z_shift(step):
    return [(i, (i + step) % 4) for i in range(4)]


def on_exp(value, pairs):
    return lax.ppermute(value, "exp", pairs)


def dot(left, right, dims, precision=None):
    return lax.dot_general(
        left, right, (dims, ((), ())), precision=precision, preferred_element_type=f32
    )


def call(body, outs, *args, scratch=(), smem=1, after=(), flops=0, bytes_accessed=0):
    count = len(args)
    specs = [
        pl.BlockSpec(memory_space=pltpu.SMEM) if i < smem else pl.BlockSpec()
        for i in range(count)
    ]
    specs += [pl.BlockSpec(memory_space=pl.ANY) for _ in after]

    def run(*refs):
        body(*refs[:count], *refs[count + len(after) :])

    return pl.pallas_call(
        run,
        out_shape=[jax.ShapeDtypeStruct(shape, kind) for shape, kind in outs],
        in_specs=specs,
        out_specs=[pl.BlockSpec() for _ in outs],
        scratch_shapes=list(scratch),
        compiler_params=pltpu.CompilerParams(vmem_limit_bytes=60 * 1024 * 1024),
        cost_estimate=pl.CostEstimate(
            flops=flops, bytes_accessed=bytes_accessed, transcendentals=0
        ),
    )(*args, *after)


def pack_weights(query, key, value, out, router, attn_gain, ffn_gain, bias, packed):
    same = lax.broadcasted_iota(jnp.int32, (24, 24), 0) == lax.broadcasted_iota(
        jnp.int32, (24, 24), 1
    )

    def column(row):
        spread = jnp.broadcast_to(row[...].astype(f32), (24, 24))
        return jnp.sum(jnp.where(same, spread, 0.0), axis=1, keepdims=True)

    first = lax.broadcasted_iota(jnp.int32, (24, HEADS), 0) == 0
    table = jnp.where(first, jnp.broadcast_to(bias[...].astype(f32), (24, HEADS)), 0.0)
    extra = jnp.concatenate(
        [
            router[...].astype(f32),
            column(ffn_gain),
            column(attn_gain),
            table,
            jnp.zeros((24, 128 - AT_BIAS - HEADS), f32),
        ],
        axis=1,
    ).astype(bf16)
    for core in range(2):
        columns = slice(core * HALF, (core + 1) * HALF)
        half = jnp.concatenate(
            [query[:, columns], key[:, columns], value[:, columns], out[:, columns], extra], axis=1
        )
        for chip in range(16):
            packed[2 * chip + core] = half


def sum_parts(parts, own):
    for core in range(2):
        total = parts[core].astype(f32)
        for chip in range(1, 16):
            total = total + parts[2 * chip + core].astype(f32)
        own[:, core * SENT : (core + 1) * SENT] = total.astype(bf16)


def diagonal_buckets():
    lane = lax.broadcasted_iota(jnp.int32, (8, 512), 1)
    row = lax.broadcasted_iota(jnp.int32, (8, 512), 0)
    relative = lane - row - 255
    distance = jnp.abs(relative)
    far = jnp.full((8, 512), 8, jnp.int32)
    for mark in reach_marks:
        far = far + (distance >= mark).astype(jnp.int32)
    return jnp.where(distance < 8, distance, far) + jnp.where(relative > 0, 16, 0)


def bucket_hot(buckets, row):
    which = lax.broadcasted_iota(jnp.int32, (BUCKETS, 512), 0)
    return (which == jnp.broadcast_to(buckets[row : row + 1], (BUCKETS, 512))).astype(f32)


def owner_rows():
    row = lax.broadcasted_iota(jnp.int32, (BUCKETS, D), 0)
    column = lax.broadcasted_iota(jnp.int32, (BUCKETS, D), 1)
    return (column == row * 24).astype(bf16)


def gain_row(extra, lane):
    pick = (lax.broadcasted_iota(jnp.int32, (8, 128), 1) == lane).astype(bf16)
    return dot(pick, extra, NT)[0:1]


def inverse_rms(values):
    return lax.rsqrt(jnp.mean(values * values, axis=-1, keepdims=True) + eps)


def attention_forward(pos, x_own, x_other, doc_col, doc_row, weights, *refs):
    extras, out_half, attn_in, projected, probs, attended_own, attended_other, base = refs
    extra = weights[:, SENT - 128 :]
    extras[...] = extra
    out_half[...] = weights[:, QKV : QKV + HALF]
    gain = gain_row(extra, AT_ATTN)
    head = lax.broadcasted_iota(jnp.int32, (128, 16), 1)
    moved = (lax.broadcasted_iota(jnp.int32, (128, 16), 0) == head + AT_BIAS).astype(bf16)
    table = dot(dot(extra, moved, NN).astype(bf16), owner_rows(), ((0,), (1,)))
    buckets = diagonal_buckets()
    for row in range(8):
        base[:, row, :] = dot(table.astype(bf16), bucket_hot(buckets, row).astype(bf16), NN)
    for block, x_ref in enumerate((x_own, x_other)):
        x = x_ref[...].astype(f32)
        attn_in[block * TOK : (block + 1) * TOK] = (x * inverse_rms(x) * gain).astype(bf16)
    for part in range(3):
        columns = slice(part * HALF, (part + 1) * HALF)
        projected[:, columns] = dot(attn_in[...], weights[:, columns], NN).astype(bf16)
    left = lax.broadcasted_iota(jnp.int32, (TOK, 128), 1) < 64
    first_head = pos[2] * (HEADS // 2)
    for block, attended in enumerate((attended_own, attended_other)):
        rows = slice(block * TOK, (block + 1) * TOK)
        same = doc_col[rows] == doc_row[block : block + 1]

        def pair_step(pair, carry):
            start = pair * 128
            queries = projected[rows, pl.ds(pl.multiple_of(start, 128), 128)]
            keys = projected[rows, pl.ds(pl.multiple_of(start + HALF, 128), 128)]
            values = projected[rows, pl.ds(pl.multiple_of(start + 2 * HALF, 128), 128)]
            results = []
            for side in range(2):
                mine = left if side == 0 else jnp.logical_not(left)
                own = jnp.where(mine, queries, jnp.zeros_like(queries))
                diagonal = base[first_head + 2 * pair + side]
                bias = jnp.concatenate(
                    [pltpu.roll(diagonal, 257 + 8 * g, 1)[:, :256] for g in range(32)], axis=0
                )
                scores = jnp.where(same, score_scale * dot(own, keys, NT) + bias, big_negative)
                top = jnp.max(scores, axis=-1, keepdims=True)
                grown = jnp.exp(scores - top)
                share = grown * (1.0 / jnp.sum(grown, axis=-1, keepdims=True))
                share = share.astype(bf16)
                probs[block * (HEADS // 2) + 2 * pair + side] = share
                results.append(dot(share, values, NN))
            attended[:, pl.ds(pl.multiple_of(start, 128), 128)] = jnp.where(
                left, results[0], results[1]
            ).astype(bf16)
            return carry

        lax.fori_loop(0, HEADS // 4, pair_step, 0)


def in_parts(value, rows):
    lane = lax.broadcasted_iota(jnp.int32, (rows, 128), 1)
    high = value.astype(bf16).astype(f32)
    middle = (value - high).astype(bf16).astype(f32)
    low = value - high - middle
    parts = jnp.where(lane == 0, high, jnp.where(lane == 1, middle, jnp.where(lane == 2, low, 0.0)))
    return parts.astype(bf16)


def from_parts(parts):
    return jnp.sum(parts.astype(f32), axis=-1, keepdims=True)


def place_grads(routes, out_grad, placer, placed_grads):
    lane = lax.broadcasted_iota(jnp.int32, (TOK, 128), 1)
    chosen = routes[...] == lane
    earlier = (
        lax.broadcasted_iota(jnp.int32, (TOK, TOK), 1)
        < lax.broadcasted_iota(jnp.int32, (TOK, TOK), 0)
    ).astype(bf16)
    counts = dot(earlier, chosen.astype(bf16), NN)
    rank = jnp.sum(jnp.where(chosen, counts, 0.0), axis=-1, keepdims=True)
    slot = routes[...] * CAP + rank.astype(jnp.int32)
    placed = (slot == lax.broadcasted_iota(jnp.int32, (TOK, SLOTS), 1)).astype(bf16)
    placer[...] = placed
    placed_grads[...] = dot(placed, out_grad[...], TN).astype(bf16)


def hold(value, until, out):
    del value, until, out


def hold_until(value, until):
    return pl.pallas_call(
        hold,
        out_shape=jax.ShapeDtypeStruct(value.shape, value.dtype),
        in_specs=[pl.BlockSpec(memory_space=pl.ANY)] * 2,
        out_specs=pl.BlockSpec(memory_space=pl.ANY),
        input_output_aliases={0: 0},
    )(value, until)


def core_halves(pos):
    own = pl.ds(pl.multiple_of(pos[2] * HALF, 128), HALF)
    other = pl.ds(pl.multiple_of((1 - pos[2]) * HALF, 128), HALF)
    return own, other


def route_forward(pos, x_ref, routes, att_own, att_other, placer, out_half, out_got, extras, *refs):
    weights, after, ffn_in, router, gate, outbound = refs
    own, other = core_halves(pos)
    weights[:, own] = out_half[...]
    weights[:, other] = out_got[...]
    extra = extras[...]
    gain = gain_row(extra, AT_FFN)
    after_attn = (
        x_ref[...].astype(f32)
        + dot(att_own[...], weights[own, :], NN)
        + dot(att_other[...], weights[other, :], NN)
    )
    after[...] = after_attn
    ffn_input = (after_attn * inverse_rms(after_attn) * gain).astype(bf16)
    ffn_in[...] = ffn_input
    lane = lax.broadcasted_iota(jnp.int32, (TOK, 128), 1)
    logits = dot(ffn_input, extra, NN)
    logits = jnp.where(lane < EXPERTS, logits, -1e30)
    grown = jnp.exp(logits - jnp.max(logits, axis=-1, keepdims=True))
    share = grown / jnp.sum(grown, axis=-1, keepdims=True)
    router[...] = share
    gates = jnp.sum(jnp.where(routes[...] == lane, share, 0.0), axis=-1, keepdims=True)
    gate[...] = gates
    outbound[:, :D] = dot(placer[...], ffn_input, TN).astype(bf16)
    outbound[:, D:] = dot(placer[...], in_parts(gates, TOK), TN).astype(bf16)


def gelu_parts(pre):
    square = pre * pre
    bend = jnp.tanh(pre * (0.7978845608028654 + 0.035677408136300125 * square))
    cdf = 0.5 + 0.5 * bend
    slope = cdf + (pre - pre * (bend * bend)) * (
        0.3989422804014327 + 0.05351611220445019 * square
    )
    return pre * cdf, slope


def expert_block(rows, mix, w_in, w_down, produced, back, total, back_total, grads):
    step = pl.program_id(0)

    @pl.when(step == 0)
    def _():
        grads[...] = (from_parts(rows[:, D:]) * mix[...].astype(f32)).astype(bf16)

    active, slope = gelu_parts(dot(rows[:, :D], w_in[0], NN))
    grad_pre = (dot(grads[...], w_down[0], NT) * slope).astype(bf16)
    forward = dot(active.astype(bf16), w_down[0], NN)
    backward = dot(grad_pre, w_in[0], NT)

    @pl.when(step == 0)
    def _():
        total[...] = forward
        back_total[...] = backward

    @pl.when(step > 0)
    def _():
        total[...] += forward
        back_total[...] += backward

    @pl.when(step == pl.num_programs(0) - 1)
    def _():
        out = total[...].astype(bf16)
        produced[...] = out
        back[:, :D] = back_total[...].astype(bf16)
        per_gate = jnp.sum(mix[...].astype(f32) * out.astype(f32), axis=-1, keepdims=True)
        back[:, D:] = in_parts(per_gate, SLOTS)


def expert_weights(pos, count, *refs):
    rows, mix = refs[:count], refs[count : 2 * count]
    w_in, w_down = refs[2 * count : 2 * count + 2]
    grad_in, grad_down = refs[-2:]
    kept = refs[2 * count + 2 : -3]
    for k in range(count):
        own = rows[k][:, :D]
        grads = (from_parts(rows[k][:, D:]) * mix[k][...].astype(f32)).astype(bf16)
        active, slope = gelu_parts(dot(own, w_in[0], NN))
        grad_pre = (dot(grads, w_down[0], NT) * slope).astype(bf16)
        to_in = dot(own, grad_pre, TN)
        to_down = dot(active.astype(bf16), grads, TN)
        if k > 0:
            grad_in[0] += to_in
            grad_down[0] += to_down
        elif kept:
            grad_in[0] = kept[0][0] + to_in
            grad_down[0] = kept[1][0] + to_down
        else:
            grad_in[0] = to_in
            grad_down[0] = to_down


BLOCK = 512
WBLOCK = 256


def run_expert(rows, mix, w_in, w_down, after):
    wide = pl.BlockSpec((SLOTS, WIDE), lambda f: (0, 0))
    whole = pl.BlockSpec((SLOTS, D), lambda f: (0, 0))

    def run(*refs):
        expert_block(*refs[:4], *refs[4 + len(after) :])

    return pl.pallas_call(
        run,
        grid=(FF // BLOCK,),
        in_specs=[
            wide,
            whole,
            pl.BlockSpec((1, D, BLOCK), lambda f: (0, 0, f)),
            pl.BlockSpec((1, BLOCK, D), lambda f: (0, f, 0)),
        ]
        + [pl.BlockSpec(memory_space=pl.ANY) for _ in after],
        out_specs=[whole, wide],
        out_shape=[
            jax.ShapeDtypeStruct((SLOTS, D), bf16),
            jax.ShapeDtypeStruct((SLOTS, WIDE), bf16),
        ],
        scratch_shapes=[
            pltpu.VMEM((SLOTS, D), f32),
            pltpu.VMEM((SLOTS, D), f32),
            pltpu.VMEM((SLOTS, D), bf16),
        ],
        compiler_params=pltpu.CompilerParams(vmem_limit_bytes=60 * 1024 * 1024),
        cost_estimate=pl.CostEstimate(
            flops=8 * SLOTS * D * FF, bytes_accessed=14 * 1024 * 1024, transcendentals=0
        ),
    )(rows, mix, w_in, w_down, *after)


def run_expert_weights(group, rows, mix, w_in, w_down, kept, after):
    steps, count = D // WBLOCK, len(rows)
    own_in = pl.BlockSpec((1, D, WBLOCK), lambda f, g: (0, 0, f))
    own_down = pl.BlockSpec((1, WBLOCK, D), lambda f, g: (0, f, 0))

    def run(pos, *refs):
        expert_weights(pos, count, *refs)

    return pl.pallas_call(
        run,
        grid_spec=pltpu.PrefetchScalarGridSpec(
            num_scalar_prefetch=1,
            grid=(steps,),
            in_specs=[
                *[pl.BlockSpec((SLOTS, WIDE), lambda f, g: (0, 0))] * count,
                *[pl.BlockSpec((SLOTS, D), lambda f, g: (0, 0))] * count,
                pl.BlockSpec((1, D, WBLOCK), lambda f, g: (0, 0, g[0] * steps + f)),
                pl.BlockSpec((1, WBLOCK, D), lambda f, g: (0, g[0] * steps + f, 0)),
                *[own_in, own_down][: len(kept)],
                pl.BlockSpec(memory_space=pl.ANY),
            ],
            out_specs=[own_in, own_down],
        ),
        out_shape=[
            jax.ShapeDtypeStruct((1, D, D), f32),
            jax.ShapeDtypeStruct((1, D, D), f32),
        ],
        input_output_aliases={2 * count + 3 + i: i for i in range(len(kept))},
        compiler_params=pltpu.CompilerParams(vmem_limit_bytes=60 * 1024 * 1024),
        cost_estimate=pl.CostEstimate(
            flops=8 * count * SLOTS * D * D, bytes_accessed=14 * 1024 * 1024, transcendentals=0
        ),
    )(group, *rows, *mix, w_in, w_down, *kept, after)


def mix_out(after, gate, placer, returned, block_out):
    expert_out = dot(placer[...], returned[...], NN)
    block_out[...] = (after[...] + gate[...] * expert_out).astype(bf16)


def norm_backward(values, grads, gain):
    inverse = inverse_rms(values)
    normed = values * inverse
    per_gain = grads * normed
    scaled = grads * gain
    back = inverse * (scaled - normed * jnp.mean(scaled * normed, axis=-1, keepdims=True))
    return back, per_gain


def column_sums(values):
    line = jnp.broadcast_to(jnp.sum(values, axis=0, keepdims=True), (8, values.shape[1]))
    first = lax.broadcasted_iota(jnp.int32, (8, 128), 0) == 0
    return dot(line, first.astype(f32), TN, HIGHEST)


def route_backward(pos, *refs):
    (routes, out_grad, att_own, att_other, after, ffn_in, router, gate, placer, grad_back, weights, extras) = refs[:12]
    grad_after, grad_own, grad_other, keep, send, whole = refs[12:]
    extra_weights = extras[...]
    gain = gain_row(extra_weights, AT_FFN)
    grad_mix = out_grad[...].astype(f32)
    after_attn = after[...]
    gates = gate[...]
    lane = lax.broadcasted_iota(jnp.int32, (TOK, 128), 1)
    grad_gate = from_parts(dot(placer[...], grad_back[:, D:], NN))
    chosen = (routes[...] == lane).astype(f32)
    grad_logits = (router[...] * (chosen - gates) * grad_gate).astype(bf16)
    router_weights = jnp.where(
        lax.broadcasted_iota(jnp.int32, (D, 128), 1) < EXPERTS, extra_weights, jnp.zeros((D, 128), bf16)
    )
    grad_ffn = dot(placer[...], grad_back[:, :D], NN) + dot(grad_logits, router_weights, NT)
    back, per_gain = norm_backward(after_attn, grad_ffn, gain)
    grad_after_attn = grad_mix + back
    grad_after[...] = grad_after_attn
    branch = grad_after_attn.astype(bf16)
    own, other = core_halves(pos)
    grad_own[...] = dot(branch, weights[own, :], NT).astype(bf16)
    grad_other[...] = dot(branch, weights[other, :], NT).astype(bf16)
    whole[own, :] = dot(att_own[...], branch, TN).astype(bf16)
    whole[other, :] = dot(att_other[...], branch, TN).astype(bf16)
    keep[:, :HALF] = whole[:, own]
    send[...] = whole[:, other]
    tall = lax.broadcasted_iota(jnp.int32, (D, 128), 1)
    extra = dot(ffn_in[...], grad_logits, TN)
    keep[:, HALF:] = jnp.where(tall == AT_FFN, column_sums(per_gain), extra).astype(bf16)


def attention_backward(pos, projected, probs, grad_own, grad_other, grad_projected, diagonals):
    left = lax.broadcasted_iota(jnp.int32, (TOK, 128), 1) < 64
    diagonals[...] = jnp.zeros_like(diagonals)
    first_head = pos[2] * (HEADS // 2)
    blocks = [slice(block * TOK, (block + 1) * TOK) for block in range(2)]

    def pair_step(pair, carry):
        start = pair * 128
        at_query = pl.ds(pl.multiple_of(start, 128), 128)
        at_key = pl.ds(pl.multiple_of(start + HALF, 128), 128)
        at_value = pl.ds(pl.multiple_of(start + 2 * HALF, 128), 128)
        to_query, to_key, to_value = [[], []], [[], []], [[], []]
        for side in range(2):
            mine = left if side == 0 else jnp.logical_not(left)
            both = jnp.zeros((TOK, TOK), f32)
            for block, rows in enumerate(blocks):
                grads = (grad_own, grad_other)[block][:, at_query]
                own = jnp.where(mine, grads, jnp.zeros_like(grads))
                share16 = probs[block * (HEADS // 2) + 2 * pair + side]
                share = share16.astype(f32)
                grad_probs = dot(own, projected[rows, at_value], NT)
                to_value[block].append(dot(share16, grads, TN))
                mixed = share * grad_probs
                grad_scores = mixed - share * jnp.sum(mixed, axis=-1, keepdims=True)
                grad16 = grad_scores.astype(bf16)
                to_query[block].append(dot(grad16, projected[rows, at_key], NN))
                to_key[block].append(dot(grad16, projected[rows, at_query], TN))
                both = both + grad16.astype(f32)
            total = jnp.zeros((8, 512), f32)
            blank = jnp.zeros((8, 256), f32)
            for g in range(32):
                lines = jnp.concatenate([both[8 * g : 8 * g + 8], blank], axis=1)
                total = total + pltpu.roll(lines, 255 - 8 * g, 1)
            diagonals[first_head + 2 * pair + side] = total
        for block, rows in enumerate(blocks):
            grad_projected[rows, at_query] = (
                score_scale * jnp.where(left, *to_query[block])
            ).astype(bf16)
            grad_projected[rows, at_key] = (
                score_scale * jnp.where(left, *to_key[block])
            ).astype(bf16)
            grad_projected[rows, at_value] = jnp.where(left, *to_value[block]).astype(bf16)
        return carry

    lax.fori_loop(0, HEADS // 4, pair_step, 0)


def weights_backward(x_own, x_other, attn_in, grad_projected, weights, diagonals, keep, got, *refs):
    whole, to_own, to_other = refs
    whole[:, :QKV] = dot(attn_in[...], grad_projected[...], TN).astype(bf16)
    whole[:, QKV : QKV + HALF] = (keep[:, :HALF].astype(f32) + got[...].astype(f32)).astype(bf16)
    sums = jnp.zeros((D, 128), f32)
    for block, (x_ref, out) in enumerate(((x_own, to_own), (x_other, to_other))):
        rows = slice(block * TOK, (block + 1) * TOK)
        grads = dot(grad_projected[rows], weights[:, :QKV], NT)
        out[...] = grads
        x = x_ref[...].astype(f32)
        sums = sums + column_sums(grads * (x * inverse_rms(x)))
    buckets = diagonal_buckets()
    per_bucket = jnp.zeros((BUCKETS, 16), f32)
    for row in range(8):
        per_bucket = per_bucket + dot(bucket_hot(buckets, row), diagonals[:, row, :], NT, HIGHEST)
    head = lax.broadcasted_iota(jnp.int32, (16, 128), 0)
    moved = (lax.broadcasted_iota(jnp.int32, (16, 128), 1) == head + AT_BIAS).astype(bf16)
    per_bucket = dot(per_bucket.astype(bf16), moved, NN)
    tall = lax.broadcasted_iota(jnp.int32, (D, 128), 1)
    extra = keep[:, HALF:].astype(f32) + dot(owner_rows(), per_bucket.astype(bf16), TN)
    whole[:, QKV + HALF :] = jnp.where(tall == AT_ATTN, sums, extra).astype(bf16)


def input_backward(x_ref, grad_after, to_own, got, extras, grad_in):
    gain = gain_row(extras[...], AT_ATTN)
    back, _ = norm_backward(x_ref[...].astype(f32), to_own[...] + got[...], gain)
    grad_in[...] = grad_after[...] + back


def sum_groups(own, one, two, three, query, key, value, out, router, attn_gain, ffn_gain, bias):
    total = (own[...].astype(f32) + two[...].astype(f32)) + (
        one[...].astype(f32) + three[...].astype(f32)
    )
    for part, target in enumerate((query, key, value, out)):
        target[:, :HALF] = total[:, part * HALF : (part + 1) * HALF]
        target[:, HALF:] = total[:, SENT + part * HALF : SENT + (part + 1) * HALF]
    extra = total[:, SENT - 128 : SENT] + total[:, 2 * SENT - 128 :]
    same = lax.broadcasted_iota(jnp.int32, (24, 24), 0) == lax.broadcasted_iota(
        jnp.int32, (24, 24), 1
    )

    def row(lane):
        spread = jnp.broadcast_to(extra[:, lane : lane + 1], (24, 24))
        return jnp.sum(jnp.where(same, spread, 0.0), axis=0, keepdims=True)

    router[...] = extra[:, :EXPERTS]
    attn_gain[...] = row(AT_ATTN)
    ffn_gain[...] = row(AT_FFN)
    bias[...] = extra[0:1, AT_BIAS : AT_BIAS + HEADS]


def on_device(
    hidden_in,
    doc_ids,
    routes,
    attn_gain,
    w_query,
    w_key,
    w_value,
    w_out,
    rel_bias,
    ffn_gain,
    w_router,
    w_in,
    w_down,
    out_grad,
):
    place = lax.axis_index("exp").astype(jnp.int32)
    pos = jnp.stack([place // 8, (place // 2) % 4, place % 2])
    group = lax.axis_index("rep").astype(jnp.int32).reshape(1)

    def over_exp(value):
        return lax.all_to_all(value, "exp", split_axis=0, concat_axis=0, tiled=True)

    def over_groups(value, step):
        return lax.ppermute(value, "rep", z_shift(step))

    (packed,) = call(
        pack_weights,
        [((EXPERTS, 24, SENT), bf16)],
        w_query,
        w_key,
        w_value,
        w_out,
        w_router,
        attn_gain.reshape(1, 24),
        ffn_gain.reshape(1, 24),
        rel_bias,
        smem=0,
    )
    weights1 = over_exp(packed).reshape(D, SENT)
    x_other = on_exp(hidden_in, SWAP)
    doc_row = jnp.stack([doc_ids, on_exp(doc_ids, SWAP)])
    doc_col = doc_row.reshape(2 * TOK, 1)

    placer, placed_grads = call(
        place_grads,
        [((TOK, SLOTS), bf16), ((SLOTS, D), bf16)],
        routes,
        out_grad,
        smem=0,
        flops=500_000_000,
        bytes_accessed=2_000_000,
    )

    def exchange(value):
        width = value.shape[1]
        return over_exp(value.reshape(EXPERTS, CAP, width)).reshape(SLOTS, width)

    slot_mix = exchange(hold_until(placed_grads, weights1))

    extras, out_half, attn_in, projected, probs, att_own, att_send = call(
        attention_forward,
        [
            ((D, 128), bf16),
            ((D, HALF), bf16),
            ((2 * TOK, D), bf16),
            ((2 * TOK, QKV), bf16),
            ((HEADS, TOK, TOK), bf16),
            ((TOK, HALF), bf16),
            ((TOK, HALF), bf16),
        ],
        pos,
        hidden_in,
        x_other,
        doc_col,
        doc_row,
        weights1,
        scratch=[pltpu.VMEM((16, 8, 512), f32)],
        flops=9_000_000_000,
        bytes_accessed=10_000_000,
    )
    att_other = on_exp(att_send, SWAP)
    out_got = on_exp(out_half, SWAP)
    weights2, after, ffn_in, router, gate, outbound = call(
        route_forward,
        [
            ((D, D), bf16),
            ((TOK, D), f32),
            ((TOK, D), bf16),
            ((TOK, 128), f32),
            ((TOK, 1), f32),
            ((SLOTS, WIDE), bf16),
        ],
        pos,
        hidden_in,
        routes,
        att_own,
        att_other,
        placer,
        out_half,
        out_got,
        extras,
        after=[slot_mix],
        flops=3_000_000_000,
        bytes_accessed=8_000_000,
    )
    mix1, mix3 = over_groups(slot_mix, 1), over_groups(slot_mix, 3)
    slot_rows = exchange(outbound)
    rows1, rows3 = over_groups(slot_rows, 1), over_groups(slot_rows, 3)
    produced, back = run_expert(slot_rows, slot_mix, w_in, w_down, [mix1, mix3])
    grad_back = exchange(back)
    returned = exchange(produced)

    grad_after, grad_own, grad_send, keep, send = call(
        route_backward,
        [
            ((TOK, D), f32),
            ((TOK, HALF), bf16),
            ((TOK, HALF), bf16),
            ((D, HALF + 128), bf16),
            ((D, HALF), bf16),
        ],
        pos,
        routes,
        out_grad,
        att_own,
        att_other,
        after,
        ffn_in,
        router,
        gate,
        placer,
        grad_back,
        weights2,
        extras,
        scratch=[pltpu.VMEM((D, D), bf16)],
        after=[rows1, rows3],
        flops=4_000_000_000,
        bytes_accessed=10_000_000,
    )
    grad_other = on_exp(grad_send, SWAP)
    got = on_exp(send, SWAP)
    grad_projected, diagonals = call(
        attention_backward,
        [((2 * TOK, QKV), bf16), ((16, 8, 512), f32)],
        pos,
        projected,
        probs,
        grad_own,
        grad_other,
        flops=9_000_000_000,
        bytes_accessed=8_000_000,
    )
    whole, to_own, to_send = call(
        weights_backward,
        [((D, SENT), bf16), ((TOK, D), f32), ((TOK, D), f32)],
        hidden_in,
        x_other,
        attn_in,
        grad_projected,
        weights1,
        diagonals,
        keep,
        got,
        smem=0,
        flops=5_000_000_000,
        bytes_accessed=10_000_000,
    )
    parts = over_exp(hold_until(whole, returned).reshape(EXPERTS, 24, SENT))
    to_got = on_exp(to_send, SWAP)
    kept = run_expert_weights(
        group,
        [slot_rows, rows1, rows3],
        [slot_mix, mix1, mix3],
        w_in,
        w_down,
        [],
        to_send,
    )
    (grad_in,) = call(
        input_backward,
        [((TOK, D), f32)],
        hidden_in,
        grad_after,
        to_own,
        to_got,
        extras,
        smem=0,
        flops=10_000_000,
        bytes_accessed=5_000_000,
    )
    (block_out,) = call(
        mix_out,
        [((TOK, D), bf16)],
        after,
        gate,
        placer,
        returned,
        smem=0,
        after=[to_send],
        flops=200_000_000,
        bytes_accessed=3_000_000,
    )
    (own,) = call(
        sum_parts, [((24, 2 * SENT), bf16)], parts, smem=0, after=[*kept, grad_in, block_out]
    )
    grad_w_in, grad_w_down = run_expert_weights(
        group,
        [over_groups(slot_rows, 2)],
        [over_groups(slot_mix, 2)],
        w_in,
        w_down,
        kept,
        own,
    )
    others = [lax.ppermute(own, "rep", z_shift(k)) for k in (1, 2, 3)]
    (
        grad_query,
        grad_key,
        grad_value,
        grad_out,
        grad_router,
        grad_attn_gain,
        grad_ffn_gain,
        grad_rel_bias,
    ) = call(
        sum_groups,
        [((24, D), f32)] * 4
        + [((24, EXPERTS), f32), ((1, 24), f32), ((1, 24), f32), ((1, HEADS), f32)],
        own,
        *others,
        smem=0,
        after=[grad_w_in, grad_w_down],
    )
    return (
        block_out,
        grad_in,
        grad_attn_gain.reshape(24),
        grad_query,
        grad_key,
        grad_value,
        grad_out,
        grad_rel_bias,
        grad_ffn_gain.reshape(24),
        grad_router,
        grad_w_in,
        grad_w_down,
    )


def solution(mesh):
    in_specs = (
        P(("rep", "exp"), None),
        P(("rep", "exp")),
        P(("rep", "exp"), None),
        P("exp"),
        P("exp", None),
        P("exp", None),
        P("exp", None),
        P("exp", None),
        P("exp", None),
        P("exp"),
        P("exp", None),
        P("exp", None, None),
        P("exp", None, None),
        P(("rep", "exp"), None),
    )
    out_specs = (
        P(("rep", "exp"), None),
        P(("rep", "exp"), None),
        P("exp"),
        P("exp", None),
        P("exp", None),
        P("exp", None),
        P("exp", None),
        P("exp", None),
        P("exp"),
        P("exp", None),
        P("exp", None, "rep"),
        P("exp", "rep", None),
    )
    return jax.shard_map(
        on_device, mesh=mesh, in_specs=in_specs, out_specs=out_specs, check_vma=False
    )
```

```python
import jax
import jax.numpy as jnp
from jax import lax
from jax.experimental import pallas as pl
from jax.experimental.pallas import tpu as pltpu
from jax.sharding import PartitionSpec as P

HEADS = 12
HEAD_DIM = 64
BUCKETS = 32
D = 768
FF = 3072
TOK = 256
EXPERTS = 32
CAP = 16
SLOTS = EXPERTS * CAP
HALF = D // 2
QKV = 3 * HALF
WIDE = D + 128
SENT = QKV + HALF + 128
AT_FFN = EXPERTS
AT_ATTN = EXPERTS + 1
AT_BIAS = EXPERTS + 2

eps = 1e-06
reach_marks = (12, 16, 23, 32, 46, 64, 91)
big_negative = -1000000000.0
score_scale = HEAD_DIM ** (-0.5)

f32 = jnp.float32
bf16 = jnp.bfloat16
HIGHEST = lax.Precision.HIGHEST

NN = ((1,), (0,))
NT = ((1,), (1,))
TN = ((0,), (0,))

SWAP = [(i, i ^ 1) for i in range(32)]


def z_shift(step):
    return [(i, (i + step) % 4) for i in range(4)]


def on_exp(value, pairs):
    return lax.ppermute(value, "exp", pairs)


def dot(left, right, dims, precision=None):
    return lax.dot_general(
        left, right, (dims, ((), ())), precision=precision, preferred_element_type=f32
    )


def call(body, outs, *args, scratch=(), smem=1, after=(), flops=0, bytes_accessed=0, vmem=53):
    count = len(args)
    specs = [
        pl.BlockSpec(memory_space=pltpu.SMEM) if i < smem else pl.BlockSpec()
        for i in range(count)
    ]
    specs += [pl.BlockSpec(memory_space=pl.ANY) for _ in after]

    def run(*refs):
        body(*refs[:count], *refs[count + len(after) :])

    return pl.pallas_call(
        run,
        out_shape=[jax.ShapeDtypeStruct(shape, kind) for shape, kind in outs],
        in_specs=specs,
        out_specs=[pl.BlockSpec() for _ in outs],
        scratch_shapes=list(scratch),
        compiler_params=pltpu.CompilerParams(vmem_limit_bytes=vmem * 1024 * 1024),
        cost_estimate=pl.CostEstimate(
            flops=flops, bytes_accessed=bytes_accessed, transcendentals=0
        ),
    )(*args, *after)


def pack_weights(query, key, value, out, router, attn_gain, ffn_gain, bias, packed):
    same = lax.broadcasted_iota(jnp.int32, (24, 24), 0) == lax.broadcasted_iota(
        jnp.int32, (24, 24), 1
    )

    def column(row):
        spread = jnp.broadcast_to(row[...].astype(f32), (24, 24))
        return jnp.sum(jnp.where(same, spread, 0.0), axis=1, keepdims=True)

    first = lax.broadcasted_iota(jnp.int32, (24, HEADS), 0) == 0
    table = jnp.where(first, jnp.broadcast_to(bias[...].astype(f32), (24, HEADS)), 0.0)
    extra = jnp.concatenate(
        [
            router[...].astype(f32),
            column(ffn_gain),
            column(attn_gain),
            table,
            jnp.zeros((24, 128 - AT_BIAS - HEADS), f32),
        ],
        axis=1,
    ).astype(bf16)
    for core in range(2):
        columns = slice(core * HALF, (core + 1) * HALF)
        half = jnp.concatenate(
            [query[:, columns], key[:, columns], value[:, columns], out[:, columns], extra], axis=1
        )
        for chip in range(16):
            packed[2 * chip + core] = half


def sum_parts(parts, own):
    for core in range(2):
        total = parts[core].astype(f32)
        for chip in range(1, 16):
            total = total + parts[2 * chip + core].astype(f32)
        own[:, core * SENT : (core + 1) * SENT] = total.astype(bf16)


def diagonal_buckets():
    lane = lax.broadcasted_iota(jnp.int32, (8, 512), 1)
    row = lax.broadcasted_iota(jnp.int32, (8, 512), 0)
    relative = lane - row - 255
    distance = jnp.abs(relative)
    far = jnp.full((8, 512), 8, jnp.int32)
    for mark in reach_marks:
        far = far + (distance >= mark).astype(jnp.int32)
    return jnp.where(distance < 8, distance, far) + jnp.where(relative > 0, 16, 0)


def bucket_hot(buckets, row):
    which = lax.broadcasted_iota(jnp.int32, (BUCKETS, 512), 0)
    return (which == jnp.broadcast_to(buckets[row : row + 1], (BUCKETS, 512))).astype(f32)


def owner_rows():
    row = lax.broadcasted_iota(jnp.int32, (BUCKETS, D), 0)
    column = lax.broadcasted_iota(jnp.int32, (BUCKETS, D), 1)
    return (column == row * 24).astype(bf16)


def gain_row(extra, lane):
    pick = (lax.broadcasted_iota(jnp.int32, (8, 128), 1) == lane).astype(bf16)
    return dot(pick, extra, NT)[0:1]


def inverse_rms(values):
    return lax.rsqrt(jnp.mean(values * values, axis=-1, keepdims=True) + eps)


def attention_forward(pos, x_own, x_other, doc_col, doc_row, weights, *refs):
    extras, out_half, attn_in, projected, probs, attended_own, attended_other, base = refs
    extra = weights[:, SENT - 128 :]
    extras[...] = extra
    out_half[...] = weights[:, QKV : QKV + HALF]
    gain = gain_row(extra, AT_ATTN)
    head = lax.broadcasted_iota(jnp.int32, (128, 16), 1)
    moved = (lax.broadcasted_iota(jnp.int32, (128, 16), 0) == head + AT_BIAS).astype(bf16)
    table = dot(dot(extra, moved, NN).astype(bf16), owner_rows(), ((0,), (1,)))
    buckets = diagonal_buckets()
    for row in range(8):
        base[:, row, :] = dot(table.astype(bf16), bucket_hot(buckets, row).astype(bf16), NN)
    for block, x_ref in enumerate((x_own, x_other)):
        x = x_ref[...].astype(f32)
        attn_in[block * TOK : (block + 1) * TOK] = (x * inverse_rms(x) * gain).astype(bf16)
    for part in range(3):
        columns = slice(part * HALF, (part + 1) * HALF)
        projected[:, columns] = dot(attn_in[...], weights[:, columns], NN).astype(bf16)
    left = lax.broadcasted_iota(jnp.int32, (TOK, 128), 1) < 64
    first_head = pos[2] * (HEADS // 2)
    for block, attended in enumerate((attended_own, attended_other)):
        rows = slice(block * TOK, (block + 1) * TOK)
        same = doc_col[rows] == doc_row[block : block + 1]

        def pair_step(pair, carry):
            start = pair * 128
            queries = projected[rows, pl.ds(pl.multiple_of(start, 128), 128)]
            keys = projected[rows, pl.ds(pl.multiple_of(start + HALF, 128), 128)]
            values = projected[rows, pl.ds(pl.multiple_of(start + 2 * HALF, 128), 128)]
            results = []
            for side in range(2):
                mine = left if side == 0 else jnp.logical_not(left)
                own = jnp.where(mine, queries, jnp.zeros_like(queries))
                diagonal = base[first_head + 2 * pair + side]
                bias = jnp.concatenate(
                    [pltpu.roll(diagonal, 257 + 8 * g, 1)[:, :256] for g in range(32)], axis=0
                )
                scores = jnp.where(same, score_scale * dot(own, keys, NT) + bias, big_negative)
                top = jnp.max(scores, axis=-1, keepdims=True)
                grown = jnp.exp(scores - top)
                share = grown * (1.0 / jnp.sum(grown, axis=-1, keepdims=True))
                share = share.astype(bf16)
                probs[block * (HEADS // 2) + 2 * pair + side] = share
                results.append(dot(share, values, NN))
            attended[:, pl.ds(pl.multiple_of(start, 128), 128)] = jnp.where(
                left, results[0], results[1]
            ).astype(bf16)
            return carry

        lax.fori_loop(0, HEADS // 4, pair_step, 0, unroll=True)


def in_parts(value, rows):
    lane = lax.broadcasted_iota(jnp.int32, (rows, 128), 1)
    high = value.astype(bf16).astype(f32)
    middle = (value - high).astype(bf16).astype(f32)
    low = value - high - middle
    parts = jnp.where(lane == 0, high, jnp.where(lane == 1, middle, jnp.where(lane == 2, low, 0.0)))
    return parts.astype(bf16)


def from_parts(parts):
    return jnp.sum(parts.astype(f32), axis=-1, keepdims=True)


def place_grads(routes, out_grad, placer, placed_grads):
    lane = lax.broadcasted_iota(jnp.int32, (TOK, 128), 1)
    chosen = routes[...] == lane
    earlier = (
        lax.broadcasted_iota(jnp.int32, (TOK, TOK), 1)
        < lax.broadcasted_iota(jnp.int32, (TOK, TOK), 0)
    ).astype(bf16)
    counts = dot(earlier, chosen.astype(bf16), NN)
    rank = jnp.sum(jnp.where(chosen, counts, 0.0), axis=-1, keepdims=True)
    slot = routes[...] * CAP + rank.astype(jnp.int32)
    placed = (slot == lax.broadcasted_iota(jnp.int32, (TOK, SLOTS), 1)).astype(bf16)
    placer[...] = placed
    placed_grads[...] = dot(placed, out_grad[...], TN).astype(bf16)


def hold(value, until, out):
    del value, until, out


def hold_until(value, until):
    return pl.pallas_call(
        hold,
        out_shape=jax.ShapeDtypeStruct(value.shape, value.dtype),
        in_specs=[pl.BlockSpec(memory_space=pl.ANY)] * 2,
        out_specs=pl.BlockSpec(memory_space=pl.ANY),
        input_output_aliases={0: 0},
    )(value, until)


def core_halves(pos):
    own = pl.ds(pl.multiple_of(pos[2] * HALF, 128), HALF)
    other = pl.ds(pl.multiple_of((1 - pos[2]) * HALF, 128), HALF)
    return own, other


def route_forward(pos, x_ref, routes, att_own, att_other, placer, out_half, out_got, extras, *refs):
    weights, after, ffn_in, router, gate, outbound = refs
    own, other = core_halves(pos)
    weights[:, own] = out_half[...]
    weights[:, other] = out_got[...]
    extra = extras[...]
    gain = gain_row(extra, AT_FFN)
    after_attn = (
        x_ref[...].astype(f32)
        + dot(att_own[...], weights[own, :], NN)
        + dot(att_other[...], weights[other, :], NN)
    )
    after[...] = after_attn
    ffn_input = (after_attn * inverse_rms(after_attn) * gain).astype(bf16)
    ffn_in[...] = ffn_input
    lane = lax.broadcasted_iota(jnp.int32, (TOK, 128), 1)
    logits = dot(ffn_input, extra, NN)
    logits = jnp.where(lane < EXPERTS, logits, -1e30)
    grown = jnp.exp(logits - jnp.max(logits, axis=-1, keepdims=True))
    share = grown / jnp.sum(grown, axis=-1, keepdims=True)
    router[...] = share
    gates = jnp.sum(jnp.where(routes[...] == lane, share, 0.0), axis=-1, keepdims=True)
    gate[...] = gates
    outbound[:, :D] = dot(placer[...], ffn_input, TN).astype(bf16)
    outbound[:, D:] = dot(placer[...], in_parts(gates, TOK), TN).astype(bf16)


def gelu_parts(pre):
    square = pre * pre
    bend = jnp.tanh(pre * (0.7978845608028654 + 0.035677408136300125 * square))
    cdf = 0.5 + 0.5 * bend
    slope = cdf + (pre - pre * (bend * bend)) * (
        0.3989422804014327 + 0.05351611220445019 * square
    )
    return pre * cdf, slope


def expert_block(rows, mix, w_in, w_down, produced, back, total, back_total, grads):
    step = pl.program_id(0)

    @pl.when(step == 0)
    def _():
        grads[...] = (from_parts(rows[:, D:]) * mix[...].astype(f32)).astype(bf16)

    active, slope = gelu_parts(dot(rows[:, :D], w_in[0], NN))
    grad_pre = (dot(grads[...], w_down[0], NT) * slope).astype(bf16)
    forward = dot(active.astype(bf16), w_down[0], NN)
    backward = dot(grad_pre, w_in[0], NT)

    @pl.when(step == 0)
    def _():
        total[...] = forward
        back_total[...] = backward

    @pl.when(step > 0)
    def _():
        total[...] += forward
        back_total[...] += backward

    @pl.when(step == pl.num_programs(0) - 1)
    def _():
        out = total[...].astype(bf16)
        produced[...] = out
        back[:, :D] = back_total[...].astype(bf16)
        per_gate = jnp.sum(mix[...].astype(f32) * out.astype(f32), axis=-1, keepdims=True)
        back[:, D:] = in_parts(per_gate, SLOTS)


def expert_weights(pos, count, *refs):
    rows, mix = refs[:count], refs[count : 2 * count]
    w_in, w_down = refs[2 * count : 2 * count + 2]
    grad_in, grad_down = refs[-2:]
    kept = refs[2 * count + 2 : -3]
    for k in range(count):
        own = rows[k][:, :D]
        grads = (from_parts(rows[k][:, D:]) * mix[k][...].astype(f32)).astype(bf16)
        active, slope = gelu_parts(dot(own, w_in[0], NN))
        grad_pre = (dot(grads, w_down[0], NT) * slope).astype(bf16)
        to_in = dot(own, grad_pre, TN)
        to_down = dot(active.astype(bf16), grads, TN)
        if k > 0:
            grad_in[0] += to_in
            grad_down[0] += to_down
        elif kept:
            grad_in[0] = kept[0][0] + to_in
            grad_down[0] = kept[1][0] + to_down
        else:
            grad_in[0] = to_in
            grad_down[0] = to_down


BLOCK = 512
WBLOCK = 256


def run_expert(rows, mix, w_in, w_down, after):
    wide = pl.BlockSpec((SLOTS, WIDE), lambda f: (0, 0))
    whole = pl.BlockSpec((SLOTS, D), lambda f: (0, 0))

    def run(*refs):
        expert_block(*refs[:4], *refs[4 + len(after) :])

    return pl.pallas_call(
        run,
        grid=(FF // BLOCK,),
        in_specs=[
            wide,
            whole,
            pl.BlockSpec((1, D, BLOCK), lambda f: (0, 0, f)),
            pl.BlockSpec((1, BLOCK, D), lambda f: (0, f, 0)),
        ]
        + [pl.BlockSpec(memory_space=pl.ANY) for _ in after],
        out_specs=[whole, wide],
        out_shape=[
            jax.ShapeDtypeStruct((SLOTS, D), bf16),
            jax.ShapeDtypeStruct((SLOTS, WIDE), bf16),
        ],
        scratch_shapes=[
            pltpu.VMEM((SLOTS, D), f32),
            pltpu.VMEM((SLOTS, D), f32),
            pltpu.VMEM((SLOTS, D), bf16),
        ],
        compiler_params=pltpu.CompilerParams(vmem_limit_bytes=60 * 1024 * 1024),
        cost_estimate=pl.CostEstimate(
            flops=8 * SLOTS * D * FF, bytes_accessed=14 * 1024 * 1024, transcendentals=0
        ),
    )(rows, mix, w_in, w_down, *after)


def run_expert_weights(group, rows, mix, w_in, w_down, kept, after):
    steps, count = D // WBLOCK, len(rows)
    own_in = pl.BlockSpec((1, D, WBLOCK), lambda f, g: (0, 0, f))
    own_down = pl.BlockSpec((1, WBLOCK, D), lambda f, g: (0, f, 0))

    def run(pos, *refs):
        expert_weights(pos, count, *refs)

    return pl.pallas_call(
        run,
        grid_spec=pltpu.PrefetchScalarGridSpec(
            num_scalar_prefetch=1,
            grid=(steps,),
            in_specs=[
                *[pl.BlockSpec((SLOTS, WIDE), lambda f, g: (0, 0))] * count,
                *[pl.BlockSpec((SLOTS, D), lambda f, g: (0, 0))] * count,
                pl.BlockSpec((1, D, WBLOCK), lambda f, g: (0, 0, g[0] * steps + f)),
                pl.BlockSpec((1, WBLOCK, D), lambda f, g: (0, g[0] * steps + f, 0)),
                *[own_in, own_down][: len(kept)],
                pl.BlockSpec(memory_space=pl.ANY),
            ],
            out_specs=[own_in, own_down],
        ),
        out_shape=[
            jax.ShapeDtypeStruct((1, D, D), f32),
            jax.ShapeDtypeStruct((1, D, D), f32),
        ],
        input_output_aliases={2 * count + 3 + i: i for i in range(len(kept))},
        compiler_params=pltpu.CompilerParams(vmem_limit_bytes=60 * 1024 * 1024),
        cost_estimate=pl.CostEstimate(
            flops=8 * count * SLOTS * D * D, bytes_accessed=14 * 1024 * 1024, transcendentals=0
        ),
    )(group, *rows, *mix, w_in, w_down, *kept, after)


def mix_out(after, gate, placer, returned, block_out):
    expert_out = dot(placer[...], returned[...], NN)
    block_out[...] = (after[...] + gate[...] * expert_out).astype(bf16)


def norm_backward(values, grads, gain):
    inverse = inverse_rms(values)
    normed = values * inverse
    per_gain = grads * normed
    scaled = grads * gain
    back = inverse * (scaled - normed * jnp.mean(scaled * normed, axis=-1, keepdims=True))
    return back, per_gain


def column_sums(values):
    line = jnp.broadcast_to(jnp.sum(values, axis=0, keepdims=True), (8, values.shape[1]))
    first = lax.broadcasted_iota(jnp.int32, (8, 128), 0) == 0
    return dot(line, first.astype(f32), TN, HIGHEST)


def route_backward(pos, *refs):
    (routes, out_grad, att_own, att_other, after, ffn_in, router, gate, placer, grad_back, weights, extras) = refs[:12]
    grad_after, grad_own, grad_other, keep, send, whole = refs[12:]
    extra_weights = extras[...]
    gain = gain_row(extra_weights, AT_FFN)
    grad_mix = out_grad[...].astype(f32)
    after_attn = after[...]
    gates = gate[...]
    lane = lax.broadcasted_iota(jnp.int32, (TOK, 128), 1)
    grad_gate = from_parts(dot(placer[...], grad_back[:, D:], NN))
    chosen = (routes[...] == lane).astype(f32)
    grad_logits = (router[...] * (chosen - gates) * grad_gate).astype(bf16)
    router_weights = jnp.where(
        lax.broadcasted_iota(jnp.int32, (D, 128), 1) < EXPERTS, extra_weights, jnp.zeros((D, 128), bf16)
    )
    grad_ffn = dot(placer[...], grad_back[:, :D], NN) + dot(grad_logits, router_weights, NT)
    back, per_gain = norm_backward(after_attn, grad_ffn, gain)
    grad_after_attn = grad_mix + back
    grad_after[...] = grad_after_attn
    branch = grad_after_attn.astype(bf16)
    own, other = core_halves(pos)
    grad_own[...] = dot(branch, weights[own, :], NT).astype(bf16)
    grad_other[...] = dot(branch, weights[other, :], NT).astype(bf16)
    whole[own, :] = dot(att_own[...], branch, TN).astype(bf16)
    whole[other, :] = dot(att_other[...], branch, TN).astype(bf16)
    keep[:, :HALF] = whole[:, own]
    send[...] = whole[:, other]
    tall = lax.broadcasted_iota(jnp.int32, (D, 128), 1)
    extra = dot(ffn_in[...], grad_logits, TN)
    keep[:, HALF:] = jnp.where(tall == AT_FFN, column_sums(per_gain), extra).astype(bf16)


def attention_backward(pos, projected, probs, grad_own, grad_other, grad_projected, diagonals):
    left = lax.broadcasted_iota(jnp.int32, (TOK, 128), 1) < 64
    diagonals[...] = jnp.zeros_like(diagonals)
    first_head = pos[2] * (HEADS // 2)
    blocks = [slice(block * TOK, (block + 1) * TOK) for block in range(2)]

    def pair_step(pair, carry):
        start = pair * 128
        at_query = pl.ds(pl.multiple_of(start, 128), 128)
        at_key = pl.ds(pl.multiple_of(start + HALF, 128), 128)
        at_value = pl.ds(pl.multiple_of(start + 2 * HALF, 128), 128)
        to_query, to_key, to_value = [[], []], [[], []], [[], []]
        for side in range(2):
            mine = left if side == 0 else jnp.logical_not(left)
            both = jnp.zeros((TOK, TOK), f32)
            for block, rows in enumerate(blocks):
                grads = (grad_own, grad_other)[block][:, at_query]
                own = jnp.where(mine, grads, jnp.zeros_like(grads))
                share16 = probs[block * (HEADS // 2) + 2 * pair + side]
                share = share16.astype(f32)
                grad_probs = dot(own, projected[rows, at_value], NT)
                to_value[block].append(dot(share16, grads, TN))
                mixed = share * grad_probs
                grad_scores = mixed - share * jnp.sum(mixed, axis=-1, keepdims=True)
                grad16 = grad_scores.astype(bf16)
                to_query[block].append(dot(grad16, projected[rows, at_key], NN))
                to_key[block].append(dot(grad16, projected[rows, at_query], TN))
                both = both + grad16.astype(f32)
            total = jnp.zeros((8, 512), f32)
            blank = jnp.zeros((8, 256), f32)
            for g in range(32):
                lines = jnp.concatenate([both[8 * g : 8 * g + 8], blank], axis=1)
                total = total + pltpu.roll(lines, 255 - 8 * g, 1)
            diagonals[first_head + 2 * pair + side] = total
        for block, rows in enumerate(blocks):
            grad_projected[rows, at_query] = (
                score_scale * jnp.where(left, *to_query[block])
            ).astype(bf16)
            grad_projected[rows, at_key] = (
                score_scale * jnp.where(left, *to_key[block])
            ).astype(bf16)
            grad_projected[rows, at_value] = jnp.where(left, *to_value[block]).astype(bf16)
        return carry

    lax.fori_loop(0, HEADS // 4, pair_step, 0)


def weights_backward(attn_in, grad_projected, weights, diagonals, keep, got, whole):
    sums = jnp.zeros((D, 1), f32)
    for part in range(3):
        columns = slice(part * HALF, (part + 1) * HALF)
        grads = dot(attn_in[...], grad_projected[:, columns], TN)
        whole[:, columns] = grads.astype(bf16)
        sums = sums + jnp.sum(grads * weights[:, columns].astype(f32), axis=-1, keepdims=True)
    extra_weights = weights[:, SENT - 128 :].astype(f32)
    sums = sums / extra_weights[:, AT_ATTN : AT_ATTN + 1]
    whole[:, QKV : QKV + HALF] = (keep[:, :HALF].astype(f32) + got[...].astype(f32)).astype(bf16)
    buckets = diagonal_buckets()
    per_bucket = jnp.zeros((BUCKETS, 16), f32)
    for row in range(8):
        per_bucket = per_bucket + dot(bucket_hot(buckets, row), diagonals[:, row, :], NT, HIGHEST)
    head = lax.broadcasted_iota(jnp.int32, (16, 128), 0)
    moved = (lax.broadcasted_iota(jnp.int32, (16, 128), 1) == head + AT_BIAS).astype(bf16)
    per_bucket = dot(per_bucket.astype(bf16), moved, NN)
    tall = lax.broadcasted_iota(jnp.int32, (D, 128), 1)
    extra = keep[:, HALF:].astype(f32) + dot(owner_rows(), per_bucket.astype(bf16), TN)
    whole[:, QKV + HALF :] = jnp.where(tall == AT_ATTN, sums, extra).astype(bf16)


def input_grads(grad_projected, weights, to_own, to_other):
    for block, out in enumerate((to_own, to_other)):
        rows = slice(block * TOK, (block + 1) * TOK)
        out[...] = dot(grad_projected[rows], weights[:, :QKV], NT)


def input_backward(x_ref, grad_after, to_own, got, extras, grad_in):
    gain = gain_row(extras[...], AT_ATTN)
    back, _ = norm_backward(x_ref[...].astype(f32), to_own[...] + got[...], gain)
    grad_in[...] = grad_after[...] + back


def sum_groups(own, one, two, three, query, key, value, out, router, attn_gain, ffn_gain, bias):
    total = (own[...].astype(f32) + two[...].astype(f32)) + (
        one[...].astype(f32) + three[...].astype(f32)
    )
    for part, target in enumerate((query, key, value, out)):
        target[:, :HALF] = total[:, part * HALF : (part + 1) * HALF]
        target[:, HALF:] = total[:, SENT + part * HALF : SENT + (part + 1) * HALF]
    extra = total[:, SENT - 128 : SENT] + total[:, 2 * SENT - 128 :]
    same = lax.broadcasted_iota(jnp.int32, (24, 24), 0) == lax.broadcasted_iota(
        jnp.int32, (24, 24), 1
    )

    def row(lane):
        spread = jnp.broadcast_to(extra[:, lane : lane + 1], (24, 24))
        return jnp.sum(jnp.where(same, spread, 0.0), axis=0, keepdims=True)

    router[...] = extra[:, :EXPERTS]
    attn_gain[...] = row(AT_ATTN)
    ffn_gain[...] = row(AT_FFN)
    bias[...] = extra[0:1, AT_BIAS : AT_BIAS + HEADS]


def on_device(
    hidden_in,
    doc_ids,
    routes,
    attn_gain,
    w_query,
    w_key,
    w_value,
    w_out,
    rel_bias,
    ffn_gain,
    w_router,
    w_in,
    w_down,
    out_grad,
):
    place = lax.axis_index("exp").astype(jnp.int32)
    pos = jnp.stack([place // 8, (place // 2) % 4, place % 2])
    group = lax.axis_index("rep").astype(jnp.int32).reshape(1)

    def over_exp(value):
        return lax.all_to_all(value, "exp", split_axis=0, concat_axis=0, tiled=True)

    def over_groups(value, step):
        return lax.ppermute(value, "rep", z_shift(step))

    (packed,) = call(
        pack_weights,
        [((EXPERTS, 24, SENT), bf16)],
        w_query,
        w_key,
        w_value,
        w_out,
        w_router,
        attn_gain.reshape(1, 24),
        ffn_gain.reshape(1, 24),
        rel_bias,
        smem=0,
        vmem=60,
    )
    weights1 = over_exp(packed).reshape(D, SENT)
    x_other = on_exp(hidden_in, SWAP)
    doc_row = jnp.stack([doc_ids, on_exp(doc_ids, SWAP)])
    doc_col = doc_row.reshape(2 * TOK, 1)

    placer, placed_grads = call(
        place_grads,
        [((TOK, SLOTS), bf16), ((SLOTS, D), bf16)],
        routes,
        out_grad,
        smem=0,
        flops=500_000_000,
        bytes_accessed=2_000_000,
    )

    def exchange(value):
        width = value.shape[1]
        return over_exp(value.reshape(EXPERTS, CAP, width)).reshape(SLOTS, width)

    slot_mix = exchange(hold_until(placed_grads, weights1))

    extras, out_half, attn_in, projected, probs, att_own, att_send = call(
        attention_forward,
        [
            ((D, 128), bf16),
            ((D, HALF), bf16),
            ((2 * TOK, D), bf16),
            ((2 * TOK, QKV), bf16),
            ((HEADS, TOK, TOK), bf16),
            ((TOK, HALF), bf16),
            ((TOK, HALF), bf16),
        ],
        pos,
        hidden_in,
        x_other,
        doc_col,
        doc_row,
        weights1,
        scratch=[pltpu.VMEM((16, 8, 512), f32)],
        flops=9_000_000_000,
        bytes_accessed=10_000_000,
    )
    att_other = on_exp(att_send, SWAP)
    out_got = on_exp(out_half, SWAP)
    weights2, after, ffn_in, router, gate, outbound = call(
        route_forward,
        [
            ((D, D), bf16),
            ((TOK, D), f32),
            ((TOK, D), bf16),
            ((TOK, 128), f32),
            ((TOK, 1), f32),
            ((SLOTS, WIDE), bf16),
        ],
        pos,
        hidden_in,
        routes,
        att_own,
        att_other,
        placer,
        out_half,
        out_got,
        extras,
        after=[slot_mix],
        flops=3_000_000_000,
        bytes_accessed=8_000_000,
    )
    mix1, mix3 = over_groups(slot_mix, 1), over_groups(slot_mix, 3)
    slot_rows = exchange(outbound)
    rows1, rows3 = over_groups(slot_rows, 1), over_groups(slot_rows, 3)
    produced, back = run_expert(slot_rows, slot_mix, w_in, w_down, [mix1, mix3])
    grad_back = exchange(back)
    returned = exchange(produced)

    grad_after, grad_own, grad_send, keep, send = call(
        route_backward,
        [
            ((TOK, D), f32),
            ((TOK, HALF), bf16),
            ((TOK, HALF), bf16),
            ((D, HALF + 128), bf16),
            ((D, HALF), bf16),
        ],
        pos,
        routes,
        out_grad,
        att_own,
        att_other,
        after,
        ffn_in,
        router,
        gate,
        placer,
        grad_back,
        weights2,
        extras,
        scratch=[pltpu.VMEM((D, D), bf16)],
        after=[rows1, rows3],
        flops=4_000_000_000,
        bytes_accessed=10_000_000,
    )
    grad_other = on_exp(grad_send, SWAP)
    got = on_exp(send, SWAP)
    grad_projected, diagonals = call(
        attention_backward,
        [((2 * TOK, QKV), bf16), ((16, 8, 512), f32)],
        pos,
        projected,
        probs,
        grad_own,
        grad_other,
        flops=9_000_000_000,
        bytes_accessed=8_000_000,
    )
    (whole,) = call(
        weights_backward,
        [((D, SENT), bf16)],
        attn_in,
        grad_projected,
        weights1,
        diagonals,
        keep,
        got,
        smem=0,
        flops=3_000_000_000,
        bytes_accessed=10_000_000,
    )
    parts = over_exp(hold_until(whole, returned).reshape(EXPERTS, 24, SENT))
    to_own, to_send = call(
        input_grads,
        [((TOK, D), f32), ((TOK, D), f32)],
        grad_projected,
        weights1,
        smem=0,
        after=[returned, diagonals],
        flops=1_000_000_000,
        bytes_accessed=6_000_000,
    )
    to_got = on_exp(to_send, SWAP)
    kept = run_expert_weights(
        group,
        [slot_rows, rows1, rows3],
        [slot_mix, mix1, mix3],
        w_in,
        w_down,
        [],
        to_send,
    )
    (grad_in,) = call(
        input_backward,
        [((TOK, D), f32)],
        hidden_in,
        grad_after,
        to_own,
        to_got,
        extras,
        smem=0,
        flops=10_000_000,
        bytes_accessed=5_000_000,
    )
    (block_out,) = call(
        mix_out,
        [((TOK, D), bf16)],
        after,
        gate,
        placer,
        returned,
        smem=0,
        after=[to_send],
        flops=200_000_000,
        bytes_accessed=3_000_000,
    )
    (own,) = call(
        sum_parts, [((24, 2 * SENT), bf16)], parts, smem=0, after=[*kept, grad_in, block_out]
    )
    grad_w_in, grad_w_down = run_expert_weights(
        group,
        [over_groups(slot_rows, 2)],
        [over_groups(slot_mix, 2)],
        w_in,
        w_down,
        kept,
        own,
    )
    others = [lax.ppermute(own, "rep", z_shift(k)) for k in (1, 2, 3)]
    (
        grad_query,
        grad_key,
        grad_value,
        grad_out,
        grad_router,
        grad_attn_gain,
        grad_ffn_gain,
        grad_rel_bias,
    ) = call(
        sum_groups,
        [((24, D), f32)] * 4
        + [((24, EXPERTS), f32), ((1, 24), f32), ((1, 24), f32), ((1, HEADS), f32)],
        own,
        *others,
        smem=0,
        after=[grad_w_in, grad_w_down],
    )
    return (
        block_out,
        grad_in,
        grad_attn_gain.reshape(24),
        grad_query,
        grad_key,
        grad_value,
        grad_out,
        grad_rel_bias,
        grad_ffn_gain.reshape(24),
        grad_router,
        grad_w_in,
        grad_w_down,
    )


def solution(mesh):
    in_specs = (
        P(("rep", "exp"), None),
        P(("rep", "exp")),
        P(("rep", "exp"), None),
        P("exp"),
        P("exp", None),
        P("exp", None),
        P("exp", None),
        P("exp", None),
        P("exp", None),
        P("exp"),
        P("exp", None),
        P("exp", None, None),
        P("exp", None, None),
        P(("rep", "exp"), None),
    )
    out_specs = (
        P(("rep", "exp"), None),
        P(("rep", "exp"), None),
        P("exp"),
        P("exp", None),
        P("exp", None),
        P("exp", None),
        P("exp", None),
        P("exp", None),
        P("exp"),
        P("exp", None),
        P("exp", None, "rep"),
        P("exp", "rep", None),
    )
    return jax.shard_map(
        on_device, mesh=mesh, in_specs=in_specs, out_specs=out_specs, check_vma=False
    )
```

```python
import jax
import jax.numpy as jnp
from jax import lax
from jax.experimental import pallas as pl
from jax.experimental.pallas import tpu as pltpu
from jax.sharding import PartitionSpec as P

HEADS = 12
HEAD_DIM = 64
BUCKETS = 32
D = 768
FF = 3072
TOK = 256
EXPERTS = 32
CAP = 16
SLOTS = EXPERTS * CAP
HALF = D // 2
QKV = 3 * HALF
WIDE = D + 128
SENT = QKV + HALF + 128
AT_FFN = EXPERTS
AT_ATTN = EXPERTS + 1
AT_BIAS = EXPERTS + 2

eps = 1e-06
reach_marks = (12, 16, 23, 32, 46, 64, 91)
big_negative = -1000000000.0
score_scale = HEAD_DIM ** (-0.5)

f32 = jnp.float32
bf16 = jnp.bfloat16
HIGHEST = lax.Precision.HIGHEST

NN = ((1,), (0,))
NT = ((1,), (1,))
TN = ((0,), (0,))

SWAP = [(i, i ^ 1) for i in range(32)]


def z_shift(step):
    return [(i, (i + step) % 4) for i in range(4)]


def on_exp(value, pairs):
    return lax.ppermute(value, "exp", pairs)


def dot(left, right, dims, precision=None):
    return lax.dot_general(
        left, right, (dims, ((), ())), precision=precision, preferred_element_type=f32
    )


def call(body, outs, *args, scratch=(), smem=1, after=(), flops=0, bytes_accessed=0, vmem=52):
    count = len(args)
    specs = [
        pl.BlockSpec(memory_space=pltpu.SMEM) if i < smem else pl.BlockSpec()
        for i in range(count)
    ]
    specs += [pl.BlockSpec(memory_space=pl.ANY) for _ in after]

    def run(*refs):
        body(*refs[:count], *refs[count + len(after) :])

    return pl.pallas_call(
        run,
        out_shape=[jax.ShapeDtypeStruct(shape, kind) for shape, kind in outs],
        in_specs=specs,
        out_specs=[pl.BlockSpec() for _ in outs],
        scratch_shapes=list(scratch),
        compiler_params=pltpu.CompilerParams(vmem_limit_bytes=vmem * 1024 * 1024),
        cost_estimate=pl.CostEstimate(
            flops=flops, bytes_accessed=bytes_accessed, transcendentals=0
        ),
    )(*args, *after)


def pack_weights(query, key, value, out, router, attn_gain, ffn_gain, bias, packed):
    same = lax.broadcasted_iota(jnp.int32, (24, 24), 0) == lax.broadcasted_iota(
        jnp.int32, (24, 24), 1
    )

    def column(row):
        spread = jnp.broadcast_to(row[...].astype(f32), (24, 24))
        return jnp.sum(jnp.where(same, spread, 0.0), axis=1, keepdims=True)

    first = lax.broadcasted_iota(jnp.int32, (24, HEADS), 0) == 0
    table = jnp.where(first, jnp.broadcast_to(bias[...].astype(f32), (24, HEADS)), 0.0)
    extra = jnp.concatenate(
        [
            router[...].astype(f32),
            column(ffn_gain),
            column(attn_gain),
            table,
            jnp.zeros((24, 128 - AT_BIAS - HEADS), f32),
        ],
        axis=1,
    ).astype(bf16)
    for core in range(2):
        columns = slice(core * HALF, (core + 1) * HALF)
        half = jnp.concatenate(
            [query[:, columns], key[:, columns], value[:, columns], out[:, columns], extra], axis=1
        )
        for chip in range(16):
            packed[2 * chip + core] = half


def sum_parts(parts, own):
    for core in range(2):
        total = parts[core].astype(f32)
        for chip in range(1, 16):
            total = total + parts[2 * chip + core].astype(f32)
        own[:, core * SENT : (core + 1) * SENT] = total.astype(bf16)


def diagonal_buckets():
    lane = lax.broadcasted_iota(jnp.int32, (8, 512), 1)
    row = lax.broadcasted_iota(jnp.int32, (8, 512), 0)
    relative = lane - row - 255
    distance = jnp.abs(relative)
    far = jnp.full((8, 512), 8, jnp.int32)
    for mark in reach_marks:
        far = far + (distance >= mark).astype(jnp.int32)
    return jnp.where(distance < 8, distance, far) + jnp.where(relative > 0, 16, 0)


def bucket_hot(buckets, row):
    which = lax.broadcasted_iota(jnp.int32, (BUCKETS, 512), 0)
    return (which == jnp.broadcast_to(buckets[row : row + 1], (BUCKETS, 512))).astype(f32)


def owner_rows():
    row = lax.broadcasted_iota(jnp.int32, (BUCKETS, D), 0)
    column = lax.broadcasted_iota(jnp.int32, (BUCKETS, D), 1)
    return (column == row * 24).astype(bf16)


def gain_row(extra, lane):
    pick = (lax.broadcasted_iota(jnp.int32, (8, 128), 1) == lane).astype(bf16)
    return dot(pick, extra, NT)[0:1]


def inverse_rms(values):
    return lax.rsqrt(jnp.mean(values * values, axis=-1, keepdims=True) + eps)


def attention_forward(pos, x_own, x_other, doc_col, doc_row, weights, *refs):
    extras, out_half, attn_in, projected, probs, attended_own, attended_other, base = refs
    extra = weights[:, SENT - 128 :]
    extras[...] = extra
    out_half[...] = weights[:, QKV : QKV + HALF]
    gain = gain_row(extra, AT_ATTN)
    head = lax.broadcasted_iota(jnp.int32, (128, 16), 1)
    moved = (lax.broadcasted_iota(jnp.int32, (128, 16), 0) == head + AT_BIAS).astype(bf16)
    table = dot(dot(extra, moved, NN).astype(bf16), owner_rows(), ((0,), (1,)))
    buckets = diagonal_buckets()
    for row in range(8):
        base[:, row, :] = dot(table.astype(bf16), bucket_hot(buckets, row).astype(bf16), NN)
    for block, x_ref in enumerate((x_own, x_other)):
        x = x_ref[...].astype(f32)
        attn_in[block * TOK : (block + 1) * TOK] = (x * inverse_rms(x) * gain).astype(bf16)
    for part in range(3):
        columns = slice(part * HALF, (part + 1) * HALF)
        projected[:, columns] = dot(attn_in[...], weights[:, columns], NN).astype(bf16)
    left = lax.broadcasted_iota(jnp.int32, (TOK, 128), 1) < 64
    first_head = pos[2] * (HEADS // 2)
    for block, attended in enumerate((attended_own, attended_other)):
        rows = slice(block * TOK, (block + 1) * TOK)
        same = doc_col[rows] == doc_row[block : block + 1]

        def pair_step(pair, carry):
            start = pair * 128
            queries = projected[rows, pl.ds(pl.multiple_of(start, 128), 128)]
            keys = projected[rows, pl.ds(pl.multiple_of(start + HALF, 128), 128)]
            values = projected[rows, pl.ds(pl.multiple_of(start + 2 * HALF, 128), 128)]
            results = []
            for side in range(2):
                mine = left if side == 0 else jnp.logical_not(left)
                own = jnp.where(mine, queries, jnp.zeros_like(queries))
                diagonal = base[first_head + 2 * pair + side]
                bias = jnp.concatenate(
                    [pltpu.roll(diagonal, 257 + 8 * g, 1)[:, :256] for g in range(32)], axis=0
                )
                scores = jnp.where(same, score_scale * dot(own, keys, NT) + bias, big_negative)
                top = jnp.max(scores, axis=-1, keepdims=True)
                grown = jnp.exp(scores - top)
                share = grown * (1.0 / jnp.sum(grown, axis=-1, keepdims=True))
                share = share.astype(bf16)
                probs[block * (HEADS // 2) + 2 * pair + side] = share
                results.append(dot(share, values, NN))
            attended[:, pl.ds(pl.multiple_of(start, 128), 128)] = jnp.where(
                left, results[0], results[1]
            ).astype(bf16)
            return carry

        lax.fori_loop(0, HEADS // 4, pair_step, 0, unroll=True)


def in_parts(value, rows):
    lane = lax.broadcasted_iota(jnp.int32, (rows, 128), 1)
    high = value.astype(bf16).astype(f32)
    middle = (value - high).astype(bf16).astype(f32)
    low = value - high - middle
    parts = jnp.where(lane == 0, high, jnp.where(lane == 1, middle, jnp.where(lane == 2, low, 0.0)))
    return parts.astype(bf16)


def from_parts(parts):
    return jnp.sum(parts.astype(f32), axis=-1, keepdims=True)


def place_grads(routes, out_grad, placer, placed_grads):
    lane = lax.broadcasted_iota(jnp.int32, (TOK, 128), 1)
    chosen = routes[...] == lane
    earlier = (
        lax.broadcasted_iota(jnp.int32, (TOK, TOK), 1)
        < lax.broadcasted_iota(jnp.int32, (TOK, TOK), 0)
    ).astype(bf16)
    counts = dot(earlier, chosen.astype(bf16), NN)
    rank = jnp.sum(jnp.where(chosen, counts, 0.0), axis=-1, keepdims=True)
    slot = routes[...] * CAP + rank.astype(jnp.int32)
    placed = (slot == lax.broadcasted_iota(jnp.int32, (TOK, SLOTS), 1)).astype(bf16)
    placer[...] = placed
    placed_grads[...] = dot(placed, out_grad[...], TN).astype(bf16)


def hold(value, until, out):
    del value, until, out


def hold_until(value, until):
    return pl.pallas_call(
        hold,
        out_shape=jax.ShapeDtypeStruct(value.shape, value.dtype),
        in_specs=[pl.BlockSpec(memory_space=pl.ANY)] * 2,
        out_specs=pl.BlockSpec(memory_space=pl.ANY),
        input_output_aliases={0: 0},
    )(value, until)


def core_halves(pos):
    own = pl.ds(pl.multiple_of(pos[2] * HALF, 128), HALF)
    other = pl.ds(pl.multiple_of((1 - pos[2]) * HALF, 128), HALF)
    return own, other


def route_forward(pos, x_ref, routes, att_own, att_other, placer, out_half, out_got, extras, *refs):
    weights, after, ffn_in, router, gate, outbound = refs
    own, other = core_halves(pos)
    weights[:, own] = out_half[...]
    weights[:, other] = out_got[...]
    extra = extras[...]
    gain = gain_row(extra, AT_FFN)
    after_attn = (
        x_ref[...].astype(f32)
        + dot(att_own[...], weights[own, :], NN)
        + dot(att_other[...], weights[other, :], NN)
    )
    after[...] = after_attn
    ffn_input = (after_attn * inverse_rms(after_attn) * gain).astype(bf16)
    ffn_in[...] = ffn_input
    lane = lax.broadcasted_iota(jnp.int32, (TOK, 128), 1)
    logits = dot(ffn_input, extra, NN)
    logits = jnp.where(lane < EXPERTS, logits, -1e30)
    grown = jnp.exp(logits - jnp.max(logits, axis=-1, keepdims=True))
    share = grown / jnp.sum(grown, axis=-1, keepdims=True)
    router[...] = share
    gates = jnp.sum(jnp.where(routes[...] == lane, share, 0.0), axis=-1, keepdims=True)
    gate[...] = gates
    outbound[:, :D] = dot(placer[...], ffn_input, TN).astype(bf16)
    outbound[:, D:] = dot(placer[...], in_parts(gates, TOK), TN).astype(bf16)


def gelu_parts(pre):
    square = pre * pre
    bend = jnp.tanh(pre * (0.7978845608028654 + 0.035677408136300125 * square))
    cdf = 0.5 + 0.5 * bend
    slope = cdf + (pre - pre * (bend * bend)) * (
        0.3989422804014327 + 0.05351611220445019 * square
    )
    return pre * cdf, slope


def expert_block(rows, mix, w_in, w_down, produced, back, total, back_total, grads):
    step = pl.program_id(0)

    @pl.when(step == 0)
    def _():
        grads[...] = (from_parts(rows[:, D:]) * mix[...].astype(f32)).astype(bf16)

    active, slope = gelu_parts(dot(rows[:, :D], w_in[0], NN))
    grad_pre = (dot(grads[...], w_down[0], NT) * slope).astype(bf16)
    forward = dot(active.astype(bf16), w_down[0], NN)
    backward = dot(grad_pre, w_in[0], NT)

    @pl.when(step == 0)
    def _():
        total[...] = forward
        back_total[...] = backward

    @pl.when(step > 0)
    def _():
        total[...] += forward
        back_total[...] += backward

    @pl.when(step == pl.num_programs(0) - 1)
    def _():
        out = total[...].astype(bf16)
        produced[...] = out
        back[:, :D] = back_total[...].astype(bf16)
        per_gate = jnp.sum(mix[...].astype(f32) * out.astype(f32), axis=-1, keepdims=True)
        back[:, D:] = in_parts(per_gate, SLOTS)


def expert_weights(pos, count, *refs):
    rows, mix = refs[:count], refs[count : 2 * count]
    w_in, w_down = refs[2 * count : 2 * count + 2]
    grad_in, grad_down = refs[-2:]
    kept = refs[2 * count + 2 : -3]
    for k in range(count):
        own = rows[k][:, :D]
        grads = (from_parts(rows[k][:, D:]) * mix[k][...].astype(f32)).astype(bf16)
        active, slope = gelu_parts(dot(own, w_in[0], NN))
        grad_pre = (dot(grads, w_down[0], NT) * slope).astype(bf16)
        to_in = dot(own, grad_pre, TN)
        to_down = dot(active.astype(bf16), grads, TN)
        if k > 0:
            grad_in[0] += to_in
            grad_down[0] += to_down
        elif kept:
            grad_in[0] = kept[0][0] + to_in
            grad_down[0] = kept[1][0] + to_down
        else:
            grad_in[0] = to_in
            grad_down[0] = to_down


BLOCK = 512
WBLOCK = 256


def run_expert(rows, mix, w_in, w_down, after):
    wide = pl.BlockSpec((SLOTS, WIDE), lambda f: (0, 0))
    whole = pl.BlockSpec((SLOTS, D), lambda f: (0, 0))

    def run(*refs):
        expert_block(*refs[:4], *refs[4 + len(after) :])

    return pl.pallas_call(
        run,
        grid=(FF // BLOCK,),
        in_specs=[
            wide,
            whole,
            pl.BlockSpec((1, D, BLOCK), lambda f: (0, 0, f)),
            pl.BlockSpec((1, BLOCK, D), lambda f: (0, f, 0)),
        ]
        + [pl.BlockSpec(memory_space=pl.ANY) for _ in after],
        out_specs=[whole, wide],
        out_shape=[
            jax.ShapeDtypeStruct((SLOTS, D), bf16),
            jax.ShapeDtypeStruct((SLOTS, WIDE), bf16),
        ],
        scratch_shapes=[
            pltpu.VMEM((SLOTS, D), f32),
            pltpu.VMEM((SLOTS, D), f32),
            pltpu.VMEM((SLOTS, D), bf16),
        ],
        compiler_params=pltpu.CompilerParams(vmem_limit_bytes=60 * 1024 * 1024),
        cost_estimate=pl.CostEstimate(
            flops=8 * SLOTS * D * FF, bytes_accessed=14 * 1024 * 1024, transcendentals=0
        ),
    )(rows, mix, w_in, w_down, *after)


def run_expert_weights(group, rows, mix, w_in, w_down, kept, after):
    steps, count = D // WBLOCK, len(rows)
    own_in = pl.BlockSpec((1, D, WBLOCK), lambda f, g: (0, 0, f))
    own_down = pl.BlockSpec((1, WBLOCK, D), lambda f, g: (0, f, 0))

    def run(pos, *refs):
        expert_weights(pos, count, *refs)

    return pl.pallas_call(
        run,
        grid_spec=pltpu.PrefetchScalarGridSpec(
            num_scalar_prefetch=1,
            grid=(steps,),
            in_specs=[
                *[pl.BlockSpec((SLOTS, WIDE), lambda f, g: (0, 0))] * count,
                *[pl.BlockSpec((SLOTS, D), lambda f, g: (0, 0))] * count,
                pl.BlockSpec((1, D, WBLOCK), lambda f, g: (0, 0, g[0] * steps + f)),
                pl.BlockSpec((1, WBLOCK, D), lambda f, g: (0, g[0] * steps + f, 0)),
                *[own_in, own_down][: len(kept)],
                pl.BlockSpec(memory_space=pl.ANY),
            ],
            out_specs=[own_in, own_down],
        ),
        out_shape=[
            jax.ShapeDtypeStruct((1, D, D), f32),
            jax.ShapeDtypeStruct((1, D, D), f32),
        ],
        input_output_aliases={2 * count + 3 + i: i for i in range(len(kept))},
        compiler_params=pltpu.CompilerParams(vmem_limit_bytes=60 * 1024 * 1024),
        cost_estimate=pl.CostEstimate(
            flops=8 * count * SLOTS * D * D, bytes_accessed=14 * 1024 * 1024, transcendentals=0
        ),
    )(group, *rows, *mix, w_in, w_down, *kept, after)


def mix_out(after, gate, placer, returned, block_out):
    expert_out = dot(placer[...], returned[...], NN)
    block_out[...] = (after[...] + gate[...] * expert_out).astype(bf16)


def norm_backward(values, grads, gain):
    inverse = inverse_rms(values)
    normed = values * inverse
    per_gain = grads * normed
    scaled = grads * gain
    back = inverse * (scaled - normed * jnp.mean(scaled * normed, axis=-1, keepdims=True))
    return back, per_gain


def column_sums(values):
    line = jnp.broadcast_to(jnp.sum(values, axis=0, keepdims=True), (8, values.shape[1]))
    first = lax.broadcasted_iota(jnp.int32, (8, 128), 0) == 0
    return dot(line, first.astype(f32), TN, HIGHEST)


def route_backward(pos, *refs):
    (routes, out_grad, att_own, att_other, after, ffn_in, router, gate, placer, grad_back, weights, extras) = refs[:12]
    grad_after, grad_own, grad_other, keep, send, whole = refs[12:]
    extra_weights = extras[...]
    gain = gain_row(extra_weights, AT_FFN)
    grad_mix = out_grad[...].astype(f32)
    after_attn = after[...]
    gates = gate[...]
    lane = lax.broadcasted_iota(jnp.int32, (TOK, 128), 1)
    grad_gate = from_parts(dot(placer[...], grad_back[:, D:], NN))
    chosen = (routes[...] == lane).astype(f32)
    grad_logits = (router[...] * (chosen - gates) * grad_gate).astype(bf16)
    router_weights = jnp.where(
        lax.broadcasted_iota(jnp.int32, (D, 128), 1) < EXPERTS, extra_weights, jnp.zeros((D, 128), bf16)
    )
    grad_ffn = dot(placer[...], grad_back[:, :D], NN) + dot(grad_logits, router_weights, NT)
    back, per_gain = norm_backward(after_attn, grad_ffn, gain)
    grad_after_attn = grad_mix + back
    grad_after[...] = grad_after_attn
    branch = grad_after_attn.astype(bf16)
    own, other = core_halves(pos)
    grad_own[...] = dot(branch, weights[own, :], NT).astype(bf16)
    grad_other[...] = dot(branch, weights[other, :], NT).astype(bf16)
    whole[own, :] = dot(att_own[...], branch, TN).astype(bf16)
    whole[other, :] = dot(att_other[...], branch, TN).astype(bf16)
    keep[:, :HALF] = whole[:, own]
    send[...] = whole[:, other]
    tall = lax.broadcasted_iota(jnp.int32, (D, 128), 1)
    extra = dot(ffn_in[...], grad_logits, TN)
    keep[:, HALF:] = jnp.where(tall == AT_FFN, column_sums(per_gain), extra).astype(bf16)


def attention_backward(pos, projected, probs, grad_own, grad_other, grad_projected, diagonals):
    left = lax.broadcasted_iota(jnp.int32, (TOK, 128), 1) < 64
    diagonals[...] = jnp.zeros_like(diagonals)
    first_head = pos[2] * (HEADS // 2)
    blocks = [slice(block * TOK, (block + 1) * TOK) for block in range(2)]

    def pair_step(pair, carry):
        start = pair * 128
        at_query = pl.ds(pl.multiple_of(start, 128), 128)
        at_key = pl.ds(pl.multiple_of(start + HALF, 128), 128)
        at_value = pl.ds(pl.multiple_of(start + 2 * HALF, 128), 128)
        to_query, to_key, to_value = [[], []], [[], []], [[], []]
        for side in range(2):
            mine = left if side == 0 else jnp.logical_not(left)
            both = jnp.zeros((TOK, TOK), f32)
            for block, rows in enumerate(blocks):
                grads = (grad_own, grad_other)[block][:, at_query]
                own = jnp.where(mine, grads, jnp.zeros_like(grads))
                share16 = probs[block * (HEADS // 2) + 2 * pair + side]
                share = share16.astype(f32)
                grad_probs = dot(own, projected[rows, at_value], NT)
                to_value[block].append(dot(share16, grads, TN))
                mixed = share * grad_probs
                grad_scores = mixed - share * jnp.sum(mixed, axis=-1, keepdims=True)
                grad16 = grad_scores.astype(bf16)
                to_query[block].append(dot(grad16, projected[rows, at_key], NN))
                to_key[block].append(dot(grad16, projected[rows, at_query], TN))
                both = both + grad16.astype(f32)
            total = jnp.zeros((8, 512), f32)
            blank = jnp.zeros((8, 256), f32)
            for g in range(32):
                lines = jnp.concatenate([both[8 * g : 8 * g + 8], blank], axis=1)
                total = total + pltpu.roll(lines, 255 - 8 * g, 1)
            diagonals[first_head + 2 * pair + side] = total
        for block, rows in enumerate(blocks):
            grad_projected[rows, at_query] = (
                score_scale * jnp.where(left, *to_query[block])
            ).astype(bf16)
            grad_projected[rows, at_key] = (
                score_scale * jnp.where(left, *to_key[block])
            ).astype(bf16)
            grad_projected[rows, at_value] = jnp.where(left, *to_value[block]).astype(bf16)
        return carry

    lax.fori_loop(0, HEADS // 4, pair_step, 0)


def weights_backward(attn_in, grad_projected, weights, diagonals, keep, got, whole):
    sums = jnp.zeros((D, 1), f32)
    for part in range(3):
        columns = slice(part * HALF, (part + 1) * HALF)
        grads = dot(attn_in[...], grad_projected[:, columns], TN)
        whole[:, columns] = grads.astype(bf16)
        sums = sums + jnp.sum(grads * weights[:, columns].astype(f32), axis=-1, keepdims=True)
    extra_weights = weights[:, SENT - 128 :].astype(f32)
    sums = sums / extra_weights[:, AT_ATTN : AT_ATTN + 1]
    whole[:, QKV : QKV + HALF] = (keep[:, :HALF].astype(f32) + got[...].astype(f32)).astype(bf16)
    buckets = diagonal_buckets()
    per_bucket = jnp.zeros((BUCKETS, 16), f32)
    for row in range(8):
        per_bucket = per_bucket + dot(bucket_hot(buckets, row), diagonals[:, row, :], NT, HIGHEST)
    head = lax.broadcasted_iota(jnp.int32, (16, 128), 0)
    moved = (lax.broadcasted_iota(jnp.int32, (16, 128), 1) == head + AT_BIAS).astype(bf16)
    per_bucket = dot(per_bucket.astype(bf16), moved, NN)
    tall = lax.broadcasted_iota(jnp.int32, (D, 128), 1)
    extra = keep[:, HALF:].astype(f32) + dot(owner_rows(), per_bucket.astype(bf16), TN)
    whole[:, QKV + HALF :] = jnp.where(tall == AT_ATTN, sums, extra).astype(bf16)


def input_grads(grad_projected, weights, to_own, to_other):
    for block, out in enumerate((to_own, to_other)):
        rows = slice(block * TOK, (block + 1) * TOK)
        out[...] = dot(grad_projected[rows], weights[:, :QKV], NT)


def input_backward(x_ref, grad_after, to_own, got, extras, grad_in):
    gain = gain_row(extras[...], AT_ATTN)
    back, _ = norm_backward(x_ref[...].astype(f32), to_own[...] + got[...], gain)
    grad_in[...] = grad_after[...] + back


def sum_groups(own, one, two, three, query, key, value, out, router, attn_gain, ffn_gain, bias):
    total = (own[...].astype(f32) + two[...].astype(f32)) + (
        one[...].astype(f32) + three[...].astype(f32)
    )
    for part, target in enumerate((query, key, value, out)):
        target[:, :HALF] = total[:, part * HALF : (part + 1) * HALF]
        target[:, HALF:] = total[:, SENT + part * HALF : SENT + (part + 1) * HALF]
    extra = total[:, SENT - 128 : SENT] + total[:, 2 * SENT - 128 :]
    same = lax.broadcasted_iota(jnp.int32, (24, 24), 0) == lax.broadcasted_iota(
        jnp.int32, (24, 24), 1
    )

    def row(lane):
        spread = jnp.broadcast_to(extra[:, lane : lane + 1], (24, 24))
        return jnp.sum(jnp.where(same, spread, 0.0), axis=0, keepdims=True)

    router[...] = extra[:, :EXPERTS]
    attn_gain[...] = row(AT_ATTN)
    ffn_gain[...] = row(AT_FFN)
    bias[...] = extra[0:1, AT_BIAS : AT_BIAS + HEADS]


def on_device(
    hidden_in,
    doc_ids,
    routes,
    attn_gain,
    w_query,
    w_key,
    w_value,
    w_out,
    rel_bias,
    ffn_gain,
    w_router,
    w_in,
    w_down,
    out_grad,
):
    place = lax.axis_index("exp").astype(jnp.int32)
    pos = jnp.stack([place // 8, (place // 2) % 4, place % 2])
    group = lax.axis_index("rep").astype(jnp.int32).reshape(1)

    def over_exp(value):
        return lax.all_to_all(value, "exp", split_axis=0, concat_axis=0, tiled=True)

    def over_groups(value, step):
        return lax.ppermute(value, "rep", z_shift(step))

    (packed,) = call(
        pack_weights,
        [((EXPERTS, 24, SENT), bf16)],
        w_query,
        w_key,
        w_value,
        w_out,
        w_router,
        attn_gain.reshape(1, 24),
        ffn_gain.reshape(1, 24),
        rel_bias,
        smem=0,
        vmem=60,
    )
    weights1 = over_exp(packed).reshape(D, SENT)
    x_other = on_exp(hidden_in, SWAP)
    doc_row = jnp.stack([doc_ids, on_exp(doc_ids, SWAP)])
    doc_col = doc_row.reshape(2 * TOK, 1)

    placer, placed_grads = call(
        place_grads,
        [((TOK, SLOTS), bf16), ((SLOTS, D), bf16)],
        routes,
        out_grad,
        smem=0,
        flops=500_000_000,
        bytes_accessed=2_000_000,
    )

    def exchange(value):
        width = value.shape[1]
        return over_exp(value.reshape(EXPERTS, CAP, width)).reshape(SLOTS, width)

    slot_mix = exchange(hold_until(placed_grads, weights1))

    extras, out_half, attn_in, projected, probs, att_own, att_send = call(
        attention_forward,
        [
            ((D, 128), bf16),
            ((D, HALF), bf16),
            ((2 * TOK, D), bf16),
            ((2 * TOK, QKV), bf16),
            ((HEADS, TOK, TOK), bf16),
            ((TOK, HALF), bf16),
            ((TOK, HALF), bf16),
        ],
        pos,
        hidden_in,
        x_other,
        doc_col,
        doc_row,
        weights1,
        scratch=[pltpu.VMEM((16, 8, 512), f32)],
        flops=9_000_000_000,
        bytes_accessed=10_000_000,
    )
    att_other = on_exp(att_send, SWAP)
    out_got = on_exp(out_half, SWAP)
    weights2, after, ffn_in, router, gate, outbound = call(
        route_forward,
        [
            ((D, D), bf16),
            ((TOK, D), f32),
            ((TOK, D), bf16),
            ((TOK, 128), f32),
            ((TOK, 1), f32),
            ((SLOTS, WIDE), bf16),
        ],
        pos,
        hidden_in,
        routes,
        att_own,
        att_other,
        placer,
        out_half,
        out_got,
        extras,
        after=[slot_mix],
        flops=3_000_000_000,
        bytes_accessed=8_000_000,
    )
    mix1, mix3 = over_groups(slot_mix, 1), over_groups(slot_mix, 3)
    slot_rows = exchange(outbound)
    rows1, rows3 = over_groups(slot_rows, 1), over_groups(slot_rows, 3)
    produced, back = run_expert(slot_rows, slot_mix, w_in, w_down, [mix1, mix3])
    grad_back = exchange(back)
    returned = exchange(produced)

    grad_after, grad_own, grad_send, keep, send = call(
        route_backward,
        [
            ((TOK, D), f32),
            ((TOK, HALF), bf16),
            ((TOK, HALF), bf16),
            ((D, HALF + 128), bf16),
            ((D, HALF), bf16),
        ],
        pos,
        routes,
        out_grad,
        att_own,
        att_other,
        after,
        ffn_in,
        router,
        gate,
        placer,
        grad_back,
        weights2,
        extras,
        scratch=[pltpu.VMEM((D, D), bf16)],
        after=[rows1, rows3],
        flops=4_000_000_000,
        bytes_accessed=10_000_000,
    )
    grad_other = on_exp(grad_send, SWAP)
    got = on_exp(send, SWAP)
    grad_projected, diagonals = call(
        attention_backward,
        [((2 * TOK, QKV), bf16), ((16, 8, 512), f32)],
        pos,
        projected,
        probs,
        grad_own,
        grad_other,
        flops=9_000_000_000,
        bytes_accessed=8_000_000,
    )
    (whole,) = call(
        weights_backward,
        [((D, SENT), bf16)],
        attn_in,
        grad_projected,
        weights1,
        diagonals,
        keep,
        got,
        smem=0,
        flops=3_000_000_000,
        bytes_accessed=10_000_000,
    )
    parts = over_exp(hold_until(whole, returned).reshape(EXPERTS, 24, SENT))
    to_own, to_send = call(
        input_grads,
        [((TOK, D), f32), ((TOK, D), f32)],
        grad_projected,
        weights1,
        smem=0,
        after=[returned, diagonals],
        flops=1_000_000_000,
        bytes_accessed=6_000_000,
    )
    to_got = on_exp(to_send, SWAP)
    kept = run_expert_weights(
        group,
        [slot_rows, rows1, rows3],
        [slot_mix, mix1, mix3],
        w_in,
        w_down,
        [],
        to_send,
    )
    (grad_in,) = call(
        input_backward,
        [((TOK, D), f32)],
        hidden_in,
        grad_after,
        to_own,
        to_got,
        extras,
        smem=0,
        flops=10_000_000,
        bytes_accessed=5_000_000,
    )
    (block_out,) = call(
        mix_out,
        [((TOK, D), bf16)],
        after,
        gate,
        placer,
        returned,
        smem=0,
        after=[to_send],
        flops=200_000_000,
        bytes_accessed=3_000_000,
    )
    (own,) = call(
        sum_parts, [((24, 2 * SENT), bf16)], parts, smem=0, after=[*kept, grad_in, block_out]
    )
    grad_w_in, grad_w_down = run_expert_weights(
        group,
        [over_groups(slot_rows, 2)],
        [over_groups(slot_mix, 2)],
        w_in,
        w_down,
        kept,
        own,
    )
    others = [lax.ppermute(own, "rep", z_shift(k)) for k in (1, 2, 3)]
    (
        grad_query,
        grad_key,
        grad_value,
        grad_out,
        grad_router,
        grad_attn_gain,
        grad_ffn_gain,
        grad_rel_bias,
    ) = call(
        sum_groups,
        [((24, D), f32)] * 4
        + [((24, EXPERTS), f32), ((1, 24), f32), ((1, 24), f32), ((1, HEADS), f32)],
        own,
        *others,
        smem=0,
        after=[grad_w_in, grad_w_down],
    )
    return (
        block_out,
        grad_in,
        grad_attn_gain.reshape(24),
        grad_query,
        grad_key,
        grad_value,
        grad_out,
        grad_rel_bias,
        grad_ffn_gain.reshape(24),
        grad_router,
        grad_w_in,
        grad_w_down,
    )


def solution(mesh):
    in_specs = (
        P(("rep", "exp"), None),
        P(("rep", "exp")),
        P(("rep", "exp"), None),
        P("exp"),
        P("exp", None),
        P("exp", None),
        P("exp", None),
        P("exp", None),
        P("exp", None),
        P("exp"),
        P("exp", None),
        P("exp", None, None),
        P("exp", None, None),
        P(("rep", "exp"), None),
    )
    out_specs = (
        P(("rep", "exp"), None),
        P(("rep", "exp"), None),
        P("exp"),
        P("exp", None),
        P("exp", None),
        P("exp", None),
        P("exp", None),
        P("exp", None),
        P("exp"),
        P("exp", None),
        P("exp", None, "rep"),
        P("exp", "rep", None),
    )
    return jax.shard_map(
        on_device, mesh=mesh, in_specs=in_specs, out_specs=out_specs, check_vma=False
    )
```
